32 devices in a mesh: bank: 4 (over y, x), seg: 8 (over z, core).
Axes of the slice: x: 2, y: 2, z: 4, core: 2. Of those that a mesh axis runs over, the one named last changes fastest.
Arguments:
- strain: bfloat16 [1024, 2, 4096], P(('bank', 'seg')), may hold values from -6 to 6
- templates: float32 [12, 2, 4096], P('bank'), may hold values from -2 to 2
- inv_psd: float32 [2, 2048], replicated, may hold values from 0.2 to 5
- seg_blocks: int32 [4, 8], P('bank'), may hold values from 1 to 32, 128 in all within a row
- dest_order: int32 [4, 8], P('bank'), may hold values from 0 to 7, each once within a row
- bin_edges: int32 [12, 9], replicated, may hold values from 0 to 2048, as said below
Outputs:
- peak_snr: float32 [512, 12], P(('bank', 'seg'))
- chisq_mean: float32 [512, 12], P(('bank', 'seg'))
The draws below stay inside these ranges and needn't reach their ends.
Inputs may be any that keep to these rules, and one draw needn't show every extreme that they name: `seg_blocks`: each row sums to 128. `dest_order`: each row holds every seg index once. `bin_edges`: each row rises strictly from 0 to 2048.
All inputs are finite; a program needn't handle non-finite values.
Results may differ from the reference program's by a relative error of at most 0.0014.
Values may be sent and summed in bfloat16 or wider, within the bound.
No kernel may reach another device: no remote copies, remote signals or barrier semaphores. Data moves between devices by JAX's collectives and lax.ppermute only.
A program may use at most 64 MiB of HBM per device.

```python
import math
import jax
import jax.numpy as jnp
import numpy as np
from jax import lax

FREQ_BINS = 2048
TIME_LAGS = 64
CHI_BINS = 8
DETECTORS = 2
BLK_DEV = 16
CAPACITY = 32
TEMPLATES = 12
ALL_SLOTS = 1024
BLOCKS = 512
N_BANK = 4
N_SEG = 8


def draw_templates(key, part):
    key = jax.random.fold_in(key, 5)
    first_key, second_key = jax.random.split(key)
    shape_all = (TEMPLATES, DETECTORS, FREQ_BINS)
    phase = jax.random.uniform(first_key, shape_all, jnp.float32, -math.pi, math.pi)
    frequency = jnp.arange(FREQ_BINS, dtype=jnp.float32)
    slope = -7.0 / 6.0
    factor = jnp.exp(jax.random.uniform(second_key, shape_all, jnp.float32, -math.log(2.0), math.log(2.0)))
    amplitude = ((frequency + 16.0) / 16.0) ** slope * factor
    return jnp.concatenate([amplitude * jnp.cos(phase), amplitude * jnp.sin(phase)], axis=-1)


def draw_bin_edges(key, part):
    key = jax.random.fold_in(key, 7)
    base_width = FREQ_BINS // (2 * CHI_BINS)
    half_band = FREQ_BINS // 2
    key_list = jax.random.split(key, TEMPLATES)

    def one_row(row_key):
        cut_points = jnp.sort(jax.random.randint(row_key, (CHI_BINS - 1,), 0, half_band + 1))
        extra = jnp.concatenate([jnp.zeros((1,), jnp.int32), cut_points.astype(jnp.int32), jnp.full((1,), half_band, jnp.int32)])
        return jnp.arange(CHI_BINS + 1, dtype=jnp.int32) * base_width + extra
    return jax.vmap(one_row)(key_list)


def steps_of(own_key, extent, cuts, least, high):
    def one(position, shards_of):
        steps = jax.random.uniform(jax.random.fold_in(jax.random.fold_in(own_key, 6), position), (shards_of,), jnp.float32, least / len(cuts), high / len(cuts))
        return jnp.repeat(jnp.exp(steps), extent[position] // shards_of).reshape((-1,) + (1,) * (len(extent) - position - 1))

    factor_of = one(*cuts[0])
    for cut in cuts[1:]:
        factor_of = factor_of * one(*cut)
    return factor_of


def split_up(amount, total, limit, lean):
    weights = [(1 << 20) // math.isqrt(standing ** lean) + 1 for standing in range(2, amount + 1)]
    rest, holding = total - limit - (amount - 1), [1] * (amount - 1)
    while rest > 0:
        free = [i for i in range(amount - 1) if holding[i] < limit]
        pool, remaining = sum([weights[i] for i in free]), rest
        for i in free:
            more = min(limit - holding[i], max(1, remaining * weights[i] // pool), rest)
            holding[i] = holding[i] + more
            rest = rest - more
    return np.array([limit] + holding)


def uneven(key, amount, total, reach, lean):
    if amount == 2:
        one = jax.random.randint(key, (), max(1, total - reach), min(reach, total - 1) + 1)
        return jnp.stack([one, total - one])
    tallies = jnp.asarray(split_up(amount, total, reach, lean), jnp.int32)
    couples = (amount - 1) // 2
    source_of, sink = tallies[1:1 + 2 * couples:2], tallies[2:2 + 2 * couples:2]
    margin = jnp.minimum(source_of - 1, reach - sink)
    moved = jax.random.randint(jax.random.fold_in(key, 1), (couples,), 0, 1 << 20) % (margin + 1)
    tallies = tallies.at[1:1 + 2 * couples:2].set(source_of - moved).at[2:2 + 2 * couples:2].set(sink + moved)
    return tallies[jax.random.permutation(jax.random.fold_in(key, 2), amount)]


def scatter_about(rng, extent, width, reach, shards=(), held_as=jnp.bfloat16):
    entries = jax.random.normal(rng, extent, jnp.float32) * width
    if len(shards) > 0:
        entries = steps_of(rng, extent, shards, -0.22, 0.18) * entries
    return jnp.clip(entries, min=-reach, max=reach).astype(held_as)


def setup_inputs(seed: int = 0) -> dict:
    seeds = jax.random.split(jax.random.key(seed), 7)
    strain = scatter_about(seeds[0], (ALL_SLOTS, DETECTORS, 2 * FREQ_BINS), 1.0, 6.0, ((0, 32),))
    templates = draw_templates(jax.random.fold_in(seeds[6], 71), 0)
    inv_psd = jnp.clip(jnp.exp(jax.random.uniform(seeds[2], (DETECTORS, FREQ_BINS), jnp.float32, math.log(0.2), math.log(5.0))), 0.2, 5.0)
    seg_blocks = jax.vmap(lambda own: uneven(own, N_SEG, N_SEG * BLK_DEV, CAPACITY, 2))(jax.random.split(seeds[3], N_BANK)).reshape((N_BANK, N_SEG)).astype(jnp.int32)
    dest_order = jax.vmap(lambda own: jax.random.permutation(own, N_SEG))(jax.random.split(seeds[4], N_BANK)).reshape((N_BANK, N_SEG)).astype(jnp.int32)
    bin_edges = draw_bin_edges(jax.random.fold_in(seeds[6], 71), 0)
    return {"strain": strain, "templates": templates, "inv_psd": inv_psd, "seg_blocks": seg_blocks, "dest_order": dest_order, "bin_edges": bin_edges}


def dft_table(freq_count, lag_count):
    frequency = jnp.arange(freq_count, dtype=jnp.int32)
    lag_ids = jnp.arange(lag_count, dtype=jnp.int32)
    turns = frequency[:, None] * lag_ids[None, :] % (2 * freq_count)
    angle = turns.astype(jnp.float32) * (math.pi / freq_count)
    cosine = jnp.cos(angle)
    sine = jnp.sin(angle)
    upper = jnp.concatenate([cosine, sine], axis=1)
    lower = jnp.concatenate([-sine, cosine], axis=1)
    return jnp.concatenate([upper, lower], axis=0).astype(jnp.bfloat16)

def filter_core(blocks, templates, edge_rows, inv_psd, dft_rows):
    freq_count = inv_psd.shape[1]
    lag_count = dft_rows.shape[1] // 2
    bin_count = edge_rows.shape[1] - 1
    block_count = blocks.shape[0]
    tmpl_count = templates.shape[0]
    detectors = inv_psd.shape[0]
    spectra = blocks.astype(jnp.float32)
    strain_re = spectra[:, None, :, :freq_count]
    strain_im = spectra[:, None, :, freq_count:]
    tmpl_re = templates[None, :, :, :freq_count]
    tmpl_im = templates[None, :, :, freq_count:]
    weights = inv_psd[None, None]
    prod_re = (tmpl_re * strain_re + tmpl_im * strain_im) * weights
    prod_im = (tmpl_re * strain_im - tmpl_im * strain_re) * weights
    frequency = jnp.arange(freq_count, dtype=jnp.int32)
    member = ((frequency[None, None, :] >= edge_rows[:, :-1, None]) & (frequency[None, None, :] < edge_rows[:, 1:, None])).astype(jnp.float32)
    bin_mask = member[None, :, None]
    masked = jnp.concatenate([prod_re[:, :, :, None, :] * bin_mask, prod_im[:, :, :, None, :] * bin_mask], axis=-1).astype(jnp.bfloat16)
    flattened = masked.reshape(-1, 2 * freq_count)
    bin_series = lax.dot_general(dft_rows.astype(jnp.float32), flattened.astype(jnp.float32), (((0,), (1,)), ((), ())), precision=lax.Precision.HIGHEST)
    bin_series = bin_series.reshape(2 * lag_count, block_count, tmpl_count, detectors, bin_count)
    part_re = bin_series[:lag_count]
    part_im = bin_series[lag_count:]
    tmpl_power = (templates[..., :freq_count] ** 2 + templates[..., freq_count:] ** 2) * inv_psd[None]
    sigma_part = jnp.einsum('tdf,tpf->tdp', tmpl_power, member, precision=lax.Precision.HIGHEST)
    sigma_total = lax.optimization_barrier(jnp.sum(sigma_part, axis=-1))
    whole_re = lax.optimization_barrier(jnp.sum(part_re, axis=-1))
    whole_im = lax.optimization_barrier(jnp.sum(part_im, axis=-1))
    snr_power = lax.optimization_barrier(jnp.sum((whole_re ** 2 + whole_im ** 2) / sigma_total, axis=-1))
    peak_rows = jnp.sqrt(lax.optimization_barrier(jnp.max(snr_power, axis=0)))
    fraction = sigma_part / sigma_total[..., None]
    dev_re = part_re - fraction * whole_re[..., None]
    dev_im = part_im - fraction * whole_im[..., None]
    chi_terms = lax.optimization_barrier(jnp.sum((dev_re ** 2 + dev_im ** 2) / sigma_part, axis=(-2, -1)))
    chi_sums = lax.optimization_barrier(jnp.mean(chi_terms, axis=0)) / (2.0 * detectors * (bin_count - 1))
    return (peak_rows, chi_sums)

def source_rows(seg_blocks, dest_order):
    bank_count, seg_count = seg_blocks.shape
    starts = (jnp.cumsum(seg_blocks, axis=1) - seg_blocks).astype(jnp.int32)
    seg_ids = jnp.arange(seg_count, dtype=jnp.int32)
    residue = lax.optimization_barrier(jnp.sum(jnp.where(dest_order[:, :, None] == seg_ids[None, None, :], seg_ids[None, :, None], 0), axis=1)).astype(jnp.int32)
    slot_ids = jnp.arange(BLK_DEV, dtype=jnp.int32)
    global_ids = residue[:, :, None] + slot_ids[None, None, :] * seg_count
    anchor = (lax.optimization_barrier(jnp.sum((starts[:, None, None, :] <= global_ids[..., None]).astype(jnp.int32), axis=-1)) - 1).astype(jnp.int32)
    first_index = jnp.take_along_axis(starts, anchor.reshape(bank_count, -1), axis=1).reshape(anchor.shape)
    bank_ids = jnp.arange(bank_count, dtype=jnp.int32)
    rows_all = (bank_ids[:, None, None] * seg_count + anchor) * CAPACITY + global_ids - first_index
    return rows_all.reshape(bank_count * seg_count, BLK_DEV).astype(jnp.int32)

def reference(strain, templates, inv_psd, seg_blocks, dest_order, bin_edges):
    row_lists = source_rows(seg_blocks, dest_order)
    dft_rows = dft_table(FREQ_BINS, TIME_LAGS)

    def per_device(index_row):
        blocks = strain[index_row]
        return filter_core(blocks, templates, bin_edges, inv_psd, dft_rows)
    peak_rows, chi_sums = lax.map(per_device, row_lists)
    return (peak_rows.reshape(BLOCKS, TEMPLATES), chi_sums.reshape(BLOCKS, TEMPLATES))
```

```python
import functools

import jax
import jax.numpy as jnp
import ml_dtypes
import numpy as np
from jax import lax
from jax.experimental import pallas as pl
from jax.experimental.pallas import tpu as pltpu
from jax.sharding import PartitionSpec as P

TIME_LAGS = 64
BLK_DEV = 16
CHUNK = 128
LANES = 128
VMEM = pl.BlockSpec(memory_space=pltpu.VMEM)
SMEM = pl.BlockSpec(memory_space=pltpu.SMEM)


def dft_chunks(freq_count):
    turns = np.arange(freq_count)[:, None] * np.arange(TIME_LAGS)[None, :] % (2 * freq_count)
    angle = turns * (np.pi / freq_count)
    cosine, sine = np.cos(angle), np.sin(angle)
    upper = np.concatenate([cosine, sine], axis=1).reshape(-1, CHUNK, 2 * TIME_LAGS)
    lower = np.concatenate([-sine, cosine], axis=1).reshape(-1, CHUNK, 2 * TIME_LAGS)
    return np.concatenate([upper, lower], axis=1).astype(np.float32).astype(ml_dtypes.bfloat16)


def seg_starts(seg_ref, start_ref, seg_count):
    total = jnp.int32(0)
    for s in range(seg_count):
        start_ref[s] = total
        total = total + seg_ref[0, s]


def inverse_order(order_ref, residue_ref, seg_count):
    for r in range(seg_count):
        residue_ref[order_ref[0, r]] = jnp.int32(r)


def arrange_strain(own_ref, other_ref, order_ref, seg_ref, spectra_ref, start_ref, residue_ref, seg_count):
    seg_here = lax.axis_index("seg")
    core = seg_here % 2
    chip = seg_here // 2
    chip_count = seg_count // 2
    pair_slots = own_ref.shape[0] // seg_count
    slots = own_ref.shape[0]
    seg_starts(seg_ref, start_ref, seg_count)
    inverse_order(order_ref, residue_ref, seg_count)
    for m in range(chip_count):
        residue = residue_ref[(chip ^ m) * 2 + core]
        for side, ref in ((0, own_ref), (1, other_ref)):
            first = (residue - start_ref[chip * 2 + (core ^ side)] + 32 * seg_count) % seg_count
            for j in range(pair_slots):
                row = (m * 2 + side) * pair_slots + j
                block = ref[first + j * seg_count].astype(jnp.float32)
                spectra_ref[row : row + 1, :] = block[0:1]
                spectra_ref[slots + row : slots + row + 1, :] = block[1:2]


def weigh(tmpl_ref, psd_ref, edge_ref, first, weighted_ref, sigma_ref, frac_ref, held_ref):
    tmpl_count, detectors, width = tmpl_ref.shape
    freq_count = width // 2
    bins = edge_ref.shape[1] - 1
    psd = psd_ref[...]
    both = jnp.concatenate([psd, psd], axis=1)
    for t in range(tmpl_count):
        rows = pl.ds(t * detectors, detectors)
        held_ref[rows, :] = tmpl_ref[t]
        weighted_ref[rows, :] = tmpl_ref[t] * both
    row_ids = lax.broadcasted_iota(jnp.int32, (8, LANES), 0) // detectors
    lane_ids = lax.broadcasted_iota(jnp.int32, (8, LANES), 1)
    edges = []
    for p in range(bins + 1):
        edge = jnp.zeros((8, LANES), jnp.int32)
        for t in range(tmpl_count):
            edge = jnp.where(row_ids == t, edge_ref[first + t, p], edge)
        edges.append(edge)
    sums = [jnp.zeros((8, LANES), jnp.float32) for _ in range(bins)]
    for c in range(freq_count // LANES):
        re, im = pl.ds(c * LANES, LANES), pl.ds(freq_count + c * LANES, LANES)
        power = held_ref[:, re] * weighted_ref[:, re] + held_ref[:, im] * weighted_ref[:, im]
        below = [lane_ids + c * LANES < edges[p] for p in range(bins + 1)]
        for p in range(bins):
            sums[p] = sums[p] + jnp.where(below[p + 1] & ~below[p], power, 0.0)
    parts = [jnp.broadcast_to(jnp.sum(s, axis=1, keepdims=True), (8, LANES)) for s in sums]
    total = functools.reduce(jnp.add, parts)
    for p in range(bins):
        sigma_ref[p] = 1.0 / parts[p]
        frac_ref[p] = parts[p] / total
    sigma_ref[bins] = 1.0 / total


def filter_templates(
    spectra_ref, weighted_ref, inv_ref, frac_ref, edge_ref, first, dft_ref, series_ref, tmpl_count, out_ref, lane_step
):
    rows, width = spectra_ref.shape
    slots = rows // 2
    freq_count = width // 2
    bins = edge_ref.shape[1] - 1
    chunk_count = freq_count // CHUNK
    lane_ids = lax.broadcasted_iota(jnp.int32, (16, LANES), 1)

    def product(t, re, im, strain_re, strain_im):
        def rows_of(lanes):
            return jnp.concatenate(
                [jnp.broadcast_to(weighted_ref[2 * t + d : 2 * t + d + 1, lanes], (slots, CHUNK)) for d in range(2)],
                axis=0,
            )

        tmpl_re, tmpl_im = rows_of(re), rows_of(im)
        prod_re = tmpl_re * strain_re + tmpl_im * strain_im
        prod_im = tmpl_re * strain_im - tmpl_im * strain_re
        return jnp.concatenate([prod_re, prod_im], axis=1).astype(jnp.bfloat16)

    def masked(prod, low, high):
        member = jnp.where((lane_ids >= low) & (lane_ids < high), 1.0, 0.0).astype(jnp.bfloat16)
        member = jnp.concatenate([member] * (rows // 16), axis=0)
        return prod * jnp.concatenate([member, member], axis=1)

    def bin_before(t, bound):
        count = jnp.int32(0)
        for j in range(1, bins):
            count = count + (edge_ref[first + t, j] < bound).astype(jnp.int32)
        return count

    running = [jnp.zeros((rows, 2 * TIME_LAGS), jnp.float32) for _ in range(tmpl_count)]
    before = [jnp.int32(0) for _ in range(tmpl_count)]
    for c in range(chunk_count):
        re, im = pl.ds(c * CHUNK, CHUNK), pl.ds(freq_count + c * CHUNK, CHUNK)
        strain_re, strain_im = spectra_ref[:, re], spectra_ref[:, im]
        stack, crosses = [], []
        after = []
        for t in range(tmpl_count):
            prod = product(t, re, im, strain_re, strain_im)
            last = jnp.int32(bins - 1) if c == chunk_count - 1 else bin_before(t, (c + 1) * CHUNK)
            after.append(last)
            cross = last > before[t]
            crosses.append(cross)
            stack.append(masked(prod, 0, edge_ref[first + t, before[t] + 1] - c * CHUNK))
            stack.append(masked(prod, jnp.where(cross, edge_ref[first + t, last] - c * CHUNK, CHUNK), CHUNK))
        got = jnp.dot(jnp.concatenate(stack, axis=0), dft_ref[c], preferred_element_type=jnp.float32)
        for t in range(tmpl_count):
            ended = running[t] + got[2 * t * rows : (2 * t + 1) * rows]
            series_ref[t, before[t]] = ended
            running[t] = jnp.where(crosses[t], got[(2 * t + 1) * rows : (2 * t + 2) * rows], ended)
            before[t] = after[t]
    for t in range(tmpl_count):
        series_ref[t, bins - 1] = running[t]

    for t in range(tmpl_count):
        for p in range(1, bins - 1):
            low, high = edge_ref[first + t, p], edge_ref[first + t, p + 1]
            c = low // CHUNK

            @pl.when(high < (c + 1) * CHUNK)
            def _(t=t, p=p, low=low, high=high, c=c):
                start = pl.multiple_of(c * CHUNK, CHUNK)
                re, im = pl.ds(start, CHUNK), pl.ds(freq_count + start, CHUNK)
                prod = product(t, re, im, spectra_ref[:, re], spectra_ref[:, im])
                prod = masked(prod, low - start, high - start)
                series_ref[t, p] = jnp.dot(prod, dft_ref[c], preferred_element_type=jnp.float32)

    out_ids = lax.broadcasted_iota(jnp.int32, (slots, LANES), 1)
    out = out_ref[...]
    for t in range(tmpl_count):
        whole = series_ref[t, 0]
        for p in range(1, bins):
            whole = whole + series_ref[t, p]

        def spread(ref, p):
            return jnp.concatenate(
                [jnp.broadcast_to(ref[p, 2 * t + d : 2 * t + d + 1, :], (slots, LANES)) for d in range(2)], axis=0
            )

        chi = jnp.zeros((rows, LANES), jnp.float32)
        for p in range(bins):
            dev = series_ref[t, p] - spread(frac_ref, p) * whole
            chi = chi + dev * dev * spread(inv_ref, p)
        chi = jnp.sum(chi[:slots] + chi[slots:], axis=1, keepdims=True) / (TIME_LAGS * 2.0 * 2 * (bins - 1))
        power = whole * whole * spread(inv_ref, bins)
        power = power[:slots] + power[slots:]
        power = power + pltpu.roll(power, TIME_LAGS, 1)
        peak = jnp.sqrt(jnp.max(power, axis=1, keepdims=True))
        out = jnp.where(out_ids == first + t, peak, out)
        out = jnp.where(out_ids == first + t + lane_step, chi, out)
    out_ref[...] = out


def own_kernel(
    seg_count,
    own_ref, other_ref, tmpl_ref, psd_ref, dft_ref, order_ref, seg_ref, edge_ref,
    spectra_ref, out_ref,
    start_ref, residue_ref, held_ref, weighted_ref, sigma_ref, frac_ref, series_ref,
):
    tmpl_count = tmpl_ref.shape[0]
    first = lax.axis_index("bank") * tmpl_count
    arrange_strain(own_ref, other_ref, order_ref, seg_ref, spectra_ref, start_ref, residue_ref, seg_count)
    out_ref[...] = jnp.zeros_like(out_ref)
    weigh(tmpl_ref, psd_ref, edge_ref, first, weighted_ref, sigma_ref, frac_ref, held_ref)
    filter_templates(
        spectra_ref, weighted_ref, sigma_ref, frac_ref, edge_ref, first, dft_ref, series_ref,
        tmpl_count, out_ref, edge_ref.shape[0],
    )


def rest_kernel(group_count, part_count, *refs):
    tmpl_refs = refs[: group_count - 1]
    spectra_ref, part_ref, psd_ref, dft_ref, edge_ref = refs[group_count - 1 : group_count + 4]
    out_refs = refs[group_count + 4 : group_count + 4 + part_count]
    held_ref, weighted_ref, sigma_ref, frac_ref, series_ref, all_ref = refs[group_count + 4 + part_count :]
    tmpl_count = tmpl_refs[0].shape[0]
    bank = lax.axis_index("bank")
    all_ref[...] = part_ref[...]
    for s in range(1, group_count):
        first = (bank ^ s) * tmpl_count
        weigh(
            tmpl_refs[s - 1], psd_ref, edge_ref, first,
            weighted_ref.at[s - 1], sigma_ref.at[s - 1], frac_ref.at[s - 1], held_ref,
        )

    def one(s, _):
        first = (bank ^ (s + 1)) * tmpl_count
        filter_templates(
            spectra_ref, weighted_ref.at[s], sigma_ref.at[s], frac_ref.at[s], edge_ref, first, dft_ref, series_ref,
            tmpl_count, all_ref, edge_ref.shape[0],
        )
        return 0

    lax.fori_loop(0, group_count - 1, one, 0)
    size = out_refs[0].shape[0]
    for m in range(part_count):
        out_refs[m][...] = all_ref[m * size : (m + 1) * size, :]


def pick_kernel(seg_count, *refs):
    chip_count = seg_count // 2
    part_refs = refs[:chip_count]
    order_ref, seg_ref, peak_ref, chi_ref, start_ref, residue_ref, held_ref, rows_ref = refs[chip_count:]
    seg_here = lax.axis_index("seg")
    core, chip = seg_here % 2, seg_here // 2
    size = part_refs[0].shape[0]
    pair_slots = size // 2
    seg_starts(seg_ref, start_ref, seg_count)
    inverse_order(order_ref, residue_ref, seg_count)
    for m in range(chip_count):
        held_ref[m] = part_refs[m][...]
    for n in range(BLK_DEV):
        block = residue_ref[seg_here] + n * seg_count
        source = jnp.int32(-1)
        for s in range(seg_count):
            source = source + (start_ref[s] <= block).astype(jnp.int32)
        slot = block - start_ref[source]
        row = ((source % 2) ^ core) * pair_slots + slot // seg_count
        rows_ref[n : n + 1, :] = held_ref[(source // 2) ^ chip, pl.ds(row, 1), :]
    tmpl_total = peak_ref.shape[1]
    rows = rows_ref[...]
    peak_ref[...] = rows[:, :tmpl_total]
    chi_ref[...] = rows[:, tmpl_total : 2 * tmpl_total]


def swap(x, axis, step):
    return lax.ppermute(x, axis, [(i, i ^ step) for i in range(lax.axis_size(axis))])


def body(strain, templates, inv_psd, seg_blocks, dest_order, bin_edges):
    seg_count, bank_count = lax.axis_size("seg"), lax.axis_size("bank")
    chip_count = seg_count // 2
    slots, detectors, width = strain.shape
    freq_count = width // 2
    tmpl_total, bins = bin_edges.shape[0], bin_edges.shape[1] - 1
    tmpl_count = templates.shape[0]
    rows = detectors * slots
    dft = jnp.asarray(dft_chunks(freq_count))
    f32 = jnp.float32

    other = swap(strain, "seg", 1)
    remote = [swap(templates, "bank", s) for s in range(1, bank_count)]

    def scratch(lead):
        return [
            pltpu.VMEM((8, width), f32),
            pltpu.VMEM(lead + (8, width), f32),
            pltpu.VMEM(lead + (bins + 1, 8, LANES), f32),
            pltpu.VMEM(lead + (bins + 1, 8, LANES), f32),
            pltpu.VMEM((tmpl_count, bins, rows, 2 * TIME_LAGS), f32),
        ]

    tables = [pltpu.SMEM((seg_count,), jnp.int32), pltpu.SMEM((seg_count,), jnp.int32)]
    params = pltpu.CompilerParams(vmem_limit_bytes=40 * 1024 * 1024)
    spectra, part = pl.pallas_call(
        functools.partial(own_kernel, seg_count),
        out_shape=(jax.ShapeDtypeStruct((rows, width), f32), jax.ShapeDtypeStruct((slots, LANES), f32)),
        in_specs=[VMEM] * 5 + [SMEM] * 3,
        out_specs=(VMEM, VMEM),
        scratch_shapes=tables + scratch(()),
        compiler_params=params,
        cost_estimate=pl.CostEstimate(flops=10**9, bytes_accessed=4 * 10**6, transcendentals=0),
        name="own_templates",
    )(strain, other, templates, inv_psd, dft, dest_order, seg_blocks, bin_edges)

    size = 2 * (slots // seg_count)
    parts = pl.pallas_call(
        functools.partial(rest_kernel, bank_count, chip_count),
        out_shape=tuple(jax.ShapeDtypeStruct((size, LANES), f32) for _ in range(chip_count)),
        in_specs=[VMEM] * (bank_count - 1 + 4) + [SMEM],
        out_specs=(VMEM,) * chip_count,
        scratch_shapes=scratch((bank_count - 1,)) + [pltpu.VMEM((slots, LANES), f32)],
        compiler_params=params,
        cost_estimate=pl.CostEstimate(flops=3 * 10**9, bytes_accessed=4 * 10**6, transcendentals=0),
        name="other_templates",
    )(*remote, spectra, part, inv_psd, dft, bin_edges)

    got = [parts[0]] + [swap(parts[m], "seg", 2 * m) for m in range(1, chip_count)]
    return pl.pallas_call(
        functools.partial(pick_kernel, seg_count),
        out_shape=tuple(jax.ShapeDtypeStruct((BLK_DEV, tmpl_total), f32) for _ in range(2)),
        in_specs=[VMEM] * chip_count + [SMEM] * 2,
        out_specs=(VMEM, VMEM),
        scratch_shapes=tables + [pltpu.VMEM((chip_count, size, LANES), f32), pltpu.VMEM((BLK_DEV, LANES), f32)],
        compiler_params=params,
        name="pick_rows",
    )(*got, dest_order, seg_blocks)


def solution(mesh):
    return jax.shard_map(
        body,
        mesh=mesh,
        in_specs=(
            P(("bank", "seg"), None, None),
            P("bank", None, None),
            P(),
            P("bank", None),
            P("bank", None),
            P(),
        ),
        out_specs=(P(("bank", "seg"), None), P(("bank", "seg"), None)),
        check_vma=False,
    )
```

```python
import functools

import jax
import jax.numpy as jnp
import ml_dtypes
import numpy as np
from jax import lax
from jax.experimental import pallas as pl
from jax.experimental.pallas import tpu as pltpu
from jax.sharding import PartitionSpec as P

TIME_LAGS = 64
BLK_DEV = 16
CHUNK = 128
LANES = 128
VMEM = pl.BlockSpec(memory_space=pltpu.VMEM)
SMEM = pl.BlockSpec(memory_space=pltpu.SMEM)


def dft_chunks(freq_count):
    turns = np.arange(freq_count)[:, None] * np.arange(TIME_LAGS)[None, :] % (2 * freq_count)
    angle = turns * (np.pi / freq_count)
    cosine, sine = np.cos(angle), np.sin(angle)
    upper = np.concatenate([cosine, sine], axis=1).reshape(-1, CHUNK, 2 * TIME_LAGS)
    lower = np.concatenate([-sine, cosine], axis=1).reshape(-1, CHUNK, 2 * TIME_LAGS)
    return np.concatenate([upper, lower], axis=1).astype(np.float32).astype(ml_dtypes.bfloat16)


def tile_rows(x):
    lead, (detectors, width) = x.shape[:-2], x.shape[-2:]
    tiles = jnp.swapaxes(x.reshape(lead + (detectors, width // LANES, LANES)), -3, -2)
    return tiles.reshape(lead + (detectors * width // LANES, LANES))


def seg_starts(seg_ref, start_ref, seg_count):
    total = jnp.int32(0)
    for s in range(seg_count):
        start_ref[s] = total
        total = total + seg_ref[0, s]


def inverse_order(order_ref, residue_ref, seg_count):
    for r in range(seg_count):
        residue_ref[order_ref[0, r]] = jnp.int32(r)


def first_slot(start_ref, residue_ref, seg_count, m, side):
    seg_here = lax.axis_index("seg")
    core, chip = seg_here % 2, seg_here // 2
    start = start_ref[chip * 2 + (core ^ side)]
    residue = residue_ref[(chip ^ m) * 2 + core]
    return start, (residue - start % seg_count + seg_count) % seg_count


def arrange_strain(side, src_ref, psd_ref, spectra_ref, start_ref, residue_ref, seg_count):
    slots, tiles = src_ref.shape[0], src_ref.shape[1]
    pair_slots = slots // seg_count
    psd = psd_ref[...]
    both = jnp.concatenate([psd, psd], axis=0)
    for m in range(seg_count // 2):
        _, first = first_slot(start_ref, residue_ref, seg_count, m, side)
        for j in range(pair_slots):
            row = (m * 2 + side) * pair_slots + j
            spectra_ref[pl.ds(row, tiles, stride=slots + 1), :] = src_ref[first + j * seg_count].astype(jnp.float32) * both


def chunk_masks(group):
    shape = (group.chunks, LANES)
    lanes = lax.broadcasted_iota(jnp.int32, shape, 1)
    starts = lax.broadcasted_iota(jnp.int32, shape, 0) * CHUNK
    for t in range(group.count):
        low = high = jnp.full(shape, CHUNK, jnp.int32)
        past = [group.edge[group.first + t, p] - starts for p in range(1, group.bins)]
        here = [(q >= 0) & (q < CHUNK) for q in past]
        for q, inside in zip(past, here):
            high = jnp.where(inside, q, high)
        for q, inside in zip(reversed(past), reversed(here)):
            low = jnp.where(inside, q, low)
        group.mask[t, 0] = jnp.where(lanes < low, 1.0, 0.0)
        group.mask[t, 1] = jnp.where(lanes >= high, 1.0, 0.0)
        group.mask[t, 2] = jnp.where(high < CHUNK, 1.0, 0.0)


def sigma_rows(group, t, psd_ref):
    bins = group.bins
    tmpl = group.tmpl[t]
    half = tmpl.shape[0] // 2
    power = (tmpl[:half] * tmpl[:half] + tmpl[half:] * tmpl[half:]) * psd_ref[...]
    shape = power.shape
    ids = lax.broadcasted_iota(jnp.int32, shape, 0) // 2 * LANES + lax.broadcasted_iota(jnp.int32, shape, 1)
    below = [ids < group.edge[group.first + t, p] for p in range(1, bins)]
    parts = []
    for p in range(bins):
        if p == 0:
            member = below[0]
        elif p == bins - 1:
            member = ~below[p - 1]
        else:
            member = below[p] & ~below[p - 1]
        part = jnp.where(member, power, 0.0)
        part = functools.reduce(jnp.add, [part[i : i + 8] for i in range(0, half, 8)])
        part = part + pltpu.roll(part, 4, 0)
        part = part + pltpu.roll(part, 2, 0)
        parts.append(jnp.broadcast_to(jnp.sum(part, axis=1, keepdims=True), (8, LANES)))
    total = functools.reduce(jnp.add, parts)
    for p in range(bins):
        group.inv[t, p] = 1.0 / parts[p]
        group.frac[t, p] = parts[p] / total
    group.inv[t, bins] = 1.0 / total


class Group:
    def __init__(self, tmpl_ref, first, edge_ref, series_ref, inv_ref, frac_ref, mask_ref=None):
        self.tmpl, self.first, self.edge = tmpl_ref, first, edge_ref
        self.series, self.inv, self.frac, self.mask = series_ref, inv_ref, frac_ref, mask_ref
        self.count, self.rows, self.bins = series_ref.shape[0], series_ref.shape[2], edge_ref.shape[1] - 1
        self.chunks = series_ref.shape[1] - (self.bins - 1)

    def chunk_of(self, t, p):
        return lax.shift_right_logical(self.edge[self.first + t, p], CHUNK.bit_length() - 1)

    def inside(self, t, p):
        return self.chunk_of(t, p) == self.chunk_of(t, p + 1)


def product(group, spectra_ref, t, chunk):
    slots = group.rows // 2

    def rows_of(ref, start, step, count):
        parts = [ref[pl.ds(start + d * step, count), :] for d in range(2)]
        return jnp.concatenate([jnp.broadcast_to(part, (slots, LANES)) for part in parts], axis=0)

    tiles = (chunk, group.chunks + chunk)
    tmpl_re, tmpl_im = (rows_of(group.tmpl.at[t], tile * 2, 1, 1) for tile in tiles)
    strain_re, strain_im = (rows_of(spectra_ref, tile * 2 * (slots + 1), slots + 1, slots) for tile in tiles)
    prod_re = tmpl_re * strain_re + tmpl_im * strain_im
    prod_im = tmpl_re * strain_im - tmpl_im * strain_re
    return jnp.concatenate([prod_re, prod_im], axis=1).astype(jnp.bfloat16)


def masked(prod, member):
    member = jnp.broadcast_to(member, (16, LANES)).astype(jnp.bfloat16)
    member = jnp.concatenate([member] * (prod.shape[0] // 16), axis=0)
    return prod * jnp.concatenate([member, member], axis=1)


def add_up(group, spectra_ref, psd_ref, dft_ref, beside=()):
    chunk_masks(group)
    for t in range(group.count):
        sigma_rows(group, t, psd_ref)
    rows = group.rows
    beside = list(beside)
    gap = group.chunks // (len(beside) + 1)
    running = [jnp.zeros((rows, 2 * TIME_LAGS), jnp.float32) for _ in range(group.count)]
    for c in range(group.chunks):
        stack = []
        for t in range(group.count):
            prod = product(group, spectra_ref, t, c)
            stack.append(masked(prod, group.mask[t, 0, c : c + 1, :]))
            stack.append(masked(prod, group.mask[t, 1, c : c + 1, :]))
        got = jnp.dot(jnp.concatenate(stack, axis=0), dft_ref[c], preferred_element_type=jnp.float32)
        for t in range(group.count):
            ended = running[t] + got[2 * t * rows : (2 * t + 1) * rows]
            group.series[t, c] = ended
            cross = jnp.broadcast_to(group.mask[t, 2, c : c + 1, :], (rows, LANES)) > 0.5
            running[t] = jnp.where(cross, got[(2 * t + 1) * rows : (2 * t + 2) * rows], ended)
        if beside and c % gap == gap - 1:
            beside.pop(0)()
    for t in range(group.count):
        group.series[t, group.chunks] = running[t]
    for write in beside:
        write()

    picks = [(t, p) for t in range(group.count) for p in range(1, group.bins - 1)]
    any_inside = functools.reduce(jnp.logical_or, [group.inside(t, p) for t, p in picks])

    @pl.when(any_inside)
    def _():
        def one(i, _):
            t, p = i // (group.bins - 2), i % (group.bins - 2) + 1

            @pl.when(group.inside(t, p))
            def _():
                c, row = group.chunk_of(t, p), group.first + t
                ids = lax.broadcasted_iota(jnp.int32, (1, LANES), 1) + c * CHUNK
                member = jnp.where((ids >= group.edge[row, p]) & (ids < group.edge[row, p + 1]), 1.0, 0.0)
                prod = masked(product(group, spectra_ref, t, c), member)
                group.series[t, group.chunks + p] = jnp.dot(prod, dft_ref[c], preferred_element_type=jnp.float32)

            return 0

        lax.fori_loop(0, len(picks), one, 0)


def test_values(group, t, out_ref):
    slots, bins = group.rows // 2, group.bins
    row = group.first + t

    def spread(ref, p):
        return jnp.concatenate(
            [jnp.broadcast_to(ref[t, p, d : d + 1, :], (slots, LANES)) for d in range(2)], axis=0
        )

    series = [group.series[t, group.chunk_of(t, 1)]]
    for p in range(1, bins - 1):
        at = jnp.where(group.inside(t, p), group.chunks + p, group.chunk_of(t, p + 1))
        series.append(group.series[t, at])
    series.append(group.series[t, group.chunks])
    whole = functools.reduce(jnp.add, series)
    chi = jnp.zeros((group.rows, LANES), jnp.float32)
    for p in range(bins):
        dev = series[p] - spread(group.frac, p) * whole
        chi = chi + dev * dev * spread(group.inv, p)
    chi = jnp.sum(chi[:slots] + chi[slots:], axis=1, keepdims=True) / (TIME_LAGS * 2.0 * 2 * (bins - 1))
    power = whole * whole * spread(group.inv, bins)
    power = power[:slots] + power[slots:]
    power = power + pltpu.roll(power, TIME_LAGS, 1)
    peak = jnp.sqrt(jnp.max(power, axis=1, keepdims=True))
    out_ids = lax.broadcasted_iota(jnp.int32, (slots, LANES), 1)
    out = jnp.where(out_ids == row, peak, out_ref[...])
    out_ref[...] = jnp.where(out_ids == row + group.edge.shape[0], chi, out)


def values_of(group, out_ref):
    return [functools.partial(test_values, group, t, out_ref) for t in range(group.count)]


def own_kernel(
    seg_count,
    other_ref, own_any, tmpl_any, psd_any, dft_any, order_any, seg_any, edge_any,
    spectra_ref, dft_ref, psd_ref, series_ref, inv_ref, frac_ref,
    own_ref, tmpl_ref, order_ref, seg_ref, edge_ref, start_ref, residue_ref, mask_ref, sems,
):
    pairs = [
        (order_any, order_ref), (seg_any, seg_ref), (edge_any, edge_ref), (psd_any, psd_ref),
        (own_any, own_ref), (tmpl_any, tmpl_ref), (dft_any, dft_ref),
    ]
    copies = [pltpu.make_async_copy(src, dst, sems.at[i]) for i, (src, dst) in enumerate(pairs)]
    for copy in copies:
        copy.start()
    for copy in copies[:4]:
        copy.wait()
    seg_starts(seg_ref, start_ref, seg_count)
    inverse_order(order_ref, residue_ref, seg_count)
    arrange_strain(1, other_ref, psd_ref, spectra_ref, start_ref, residue_ref, seg_count)
    copies[4].wait()
    arrange_strain(0, own_ref, psd_ref, spectra_ref, start_ref, residue_ref, seg_count)
    copies[5].wait()
    copies[6].wait()
    first = lax.axis_index("bank") * tmpl_ref.shape[0]
    group = Group(tmpl_ref, first, edge_ref, series_ref, inv_ref, frac_ref, mask_ref)
    add_up(group, spectra_ref, psd_ref, dft_ref)


def next_kernel(
    tmpl_ref, spectra_ref, dft_ref, psd_ref, old_series_ref, old_inv_ref, old_frac_ref, edge_ref,
    out_ref, series_ref, inv_ref, frac_ref,
    mask_ref,
):
    bank = lax.axis_index("bank")
    count = tmpl_ref.shape[0]
    old = Group(None, bank * count, edge_ref, old_series_ref, old_inv_ref, old_frac_ref)
    group = Group(tmpl_ref, (bank ^ 1) * count, edge_ref, series_ref, inv_ref, frac_ref, mask_ref)
    out_ref[...] = jnp.zeros_like(out_ref)
    add_up(group, spectra_ref, psd_ref, dft_ref, values_of(old, out_ref))


def last_kernel(
    seg_count, tmpl_refs,
    spectra_ref, dft_ref, psd_ref, part_ref, old_series_ref, old_inv_ref, old_frac_ref, edge_ref, order_ref, seg_ref,
    out_refs,
    all_ref, placed_ref, start_ref, residue_ref, held,
):
    bank = lax.axis_index("bank")
    seg_starts(seg_ref, start_ref, seg_count)
    inverse_order(order_ref, residue_ref, seg_count)
    all_ref[...] = part_ref[...]
    placed_ref[...] = jnp.zeros_like(placed_ref)
    count = old_series_ref.shape[0]
    group = Group(None, (bank ^ 1) * count, edge_ref, old_series_ref, old_inv_ref, old_frac_ref)
    for s, tmpl_ref in enumerate(tmpl_refs):
        old, group = group, Group(tmpl_ref, (bank ^ (s + 2)) * count, edge_ref, *held[s])
        add_up(group, spectra_ref, psd_ref, dft_ref, values_of(old, all_ref))
    for write in values_of(group, all_ref):
        write()
    pair_slots = all_ref.shape[0] // seg_count
    seg_here = lax.axis_index("seg")
    core, chip = seg_here % 2, seg_here // 2
    ids = lax.broadcasted_iota(jnp.int32, (pair_slots, LANES), 0)
    for m in range(seg_count // 2):
        for source in range(2):
            side = core ^ source
            start, first = first_slot(start_ref, residue_ref, seg_count, m, side)
            live = (seg_ref[0, chip * 2 + source] - first + seg_count - 1) // seg_count
            values = all_ref[pl.ds((m * 2 + side) * pair_slots, pair_slots), :]
            placed_ref[m, pl.ds((start + first) // seg_count, pair_slots), :] = jnp.where(ids < live, values, 0.0)
        out_refs[m][...] = placed_ref[m, :BLK_DEV]


def add_kernel(part_refs, peak_ref, chi_ref):
    tmpl_total = peak_ref.shape[1]
    rows = functools.reduce(jnp.add, [ref[...] for ref in part_refs])
    peak_ref[...] = rows[:, :tmpl_total]
    chi_ref[...] = rows[:, tmpl_total : 2 * tmpl_total]


def swap(x, axis, step):
    return lax.ppermute(x, axis, [(i, i ^ step) for i in range(lax.axis_size(axis))])


def body(strain, templates, inv_psd, seg_blocks, dest_order, bin_edges):
    seg_count, bank_count = lax.axis_size("seg"), lax.axis_size("bank")
    chip_count = seg_count // 2
    slots, detectors, width = strain.shape
    freq_count = width // 2
    tmpl_total, bins = bin_edges.shape[0], bin_edges.shape[1] - 1
    tmpl_count = templates.shape[0]
    rows = detectors * slots
    tiles = detectors * width // LANES
    f32, i32 = jnp.float32, jnp.int32
    dft = jnp.asarray(dft_chunks(freq_count))
    psd = tile_rows(inv_psd)

    other = tile_rows(swap(strain, "seg", 1))
    remote = [tile_rows(swap(templates, "bank", s)) for s in range(1, bank_count)]

    def shape(*dims, dtype=f32):
        return jax.ShapeDtypeStruct(dims, dtype)

    chunks = freq_count // CHUNK
    sums = [(tmpl_count, chunks + bins - 1, rows, 2 * TIME_LAGS)] + [(tmpl_count, bins + 1, 8, LANES)] * 2
    sum_shapes = tuple(shape(*dims) for dims in sums)
    mask = pltpu.VMEM((tmpl_count, 3, chunks, LANES), f32)
    tables = [pltpu.SMEM((seg_count,), i32), pltpu.SMEM((seg_count,), i32)]

    def call(kernel, name, flops, **kwargs):
        return pl.pallas_call(
            kernel,
            name=name,
            cost_estimate=pl.CostEstimate(flops=flops, bytes_accessed=4 * 10**6, transcendentals=0),
            compiler_params=pltpu.CompilerParams(vmem_limit_bytes=40 * 1024 * 1024),
            **kwargs,
        )

    spectra, dft_held, psd_held, *series = call(
        functools.partial(own_kernel, seg_count),
        "own_templates",
        10**9,
        out_shape=(shape((slots + 1) * tiles, LANES), shape(*dft.shape, dtype=dft.dtype), shape(*psd.shape)) + sum_shapes,
        in_specs=[VMEM] + [pl.BlockSpec(memory_space=pltpu.HBM)] * 7,
        out_specs=(VMEM,) * 6,
        scratch_shapes=[
            pltpu.VMEM((slots, tiles, LANES), strain.dtype),
            pltpu.VMEM((tmpl_count, tiles, LANES), f32),
            pltpu.SMEM(dest_order.shape, i32),
            pltpu.SMEM(seg_blocks.shape, i32),
            pltpu.SMEM(bin_edges.shape, i32),
        ]
        + tables
        + [mask, pltpu.SemaphoreType.DMA((7,))],
    )(
        other,
        *[
            pltpu.with_memory_space_constraint(x, pltpu.HBM)
            for x in (tile_rows(strain), tile_rows(templates), psd, dft, dest_order, seg_blocks, bin_edges)
        ],
    )

    part, *series = call(
        next_kernel,
        "next_templates",
        10**9,
        out_shape=(shape(slots, LANES),) + sum_shapes,
        in_specs=[VMEM] * 7 + [SMEM],
        out_specs=(VMEM,) * 4,
        scratch_shapes=[mask],
    )(remote[0], spectra, dft_held, psd_held, *series, bin_edges)

    left = bank_count - 2

    def last(*refs):
        ins, outs, held = refs[: left + 10], refs[left + 10 : left + 10 + chip_count], refs[left + 10 + chip_count :]
        groups = [held[4 + 4 * s : 8 + 4 * s] for s in range(left)]
        last_kernel(seg_count, ins[:left], *ins[left:], outs, *held[:4], groups)

    parts = call(
        last,
        "last_templates",
        2 * 10**9,
        out_shape=(shape(BLK_DEV, LANES),) * chip_count,
        in_specs=[VMEM] * (left + 7) + [SMEM] * 3,
        out_specs=(VMEM,) * chip_count,
        scratch_shapes=[pltpu.VMEM((slots, LANES), f32), pltpu.VMEM((chip_count, BLK_DEV + 8, LANES), f32)]
        + tables
        + ([pltpu.VMEM(dims, f32) for dims in sums] + [mask]) * left,
    )(*remote[1:], spectra, dft_held, psd_held, part, *series, bin_edges, dest_order, seg_blocks)

    got = [swap(parts[m], "seg", 2 * m) for m in reversed(range(1, chip_count))] + [parts[0]]
    return call(
        lambda *refs: add_kernel(refs[:chip_count], *refs[chip_count:]),
        "add_rows",
        10**5,
        out_shape=(shape(BLK_DEV, tmpl_total),) * 2,
        in_specs=[VMEM] * chip_count,
        out_specs=(VMEM, VMEM),
    )(*got)


def solution(mesh):
    return jax.shard_map(
        body,
        mesh=mesh,
        in_specs=(
            P(("bank", "seg"), None, None),
            P("bank", None, None),
            P(),
            P("bank", None),
            P("bank", None),
            P(),
        ),
        out_specs=(P(("bank", "seg"), None), P(("bank", "seg"), None)),
        check_vma=False,
    )
```

```python
import functools

import jax
import jax.numpy as jnp
import ml_dtypes
import numpy as np
from jax import lax
from jax.experimental import pallas as pl
from jax.experimental.pallas import tpu as pltpu
from jax.sharding import PartitionSpec as P

TIME_LAGS = 64
BLK_DEV = 16
CHUNK = 128
LANES = 128
VMEM = pl.BlockSpec(memory_space=pltpu.VMEM)
SMEM = pl.BlockSpec(memory_space=pltpu.SMEM)


def dft_chunks(freq_count):
    turns = np.arange(freq_count)[:, None] * np.arange(TIME_LAGS)[None, :] % (2 * freq_count)
    angle = turns * (np.pi / freq_count)
    cosine, sine = np.cos(angle), np.sin(angle)
    upper = np.concatenate([cosine, sine], axis=1).reshape(-1, CHUNK, 2 * TIME_LAGS)
    lower = np.concatenate([-sine, cosine], axis=1).reshape(-1, CHUNK, 2 * TIME_LAGS)
    return np.concatenate([upper, lower], axis=1).astype(np.float32).astype(ml_dtypes.bfloat16)


def tile_rows(x):
    lead, (detectors, width) = x.shape[:-2], x.shape[-2:]
    tiles = jnp.swapaxes(x.reshape(lead + (detectors, width // LANES, LANES)), -3, -2)
    return tiles.reshape(lead + (detectors * width // LANES, LANES))


def core_here():
    return lax.axis_index("seg") % 2


def seg_starts(seg_ref, start_ref, seg_count, in_vmem=False):
    total = jnp.int32(0)
    for s in range(seg_count):
        start_ref[s] = total
        total = total + seg_ref[:, s : s + 1][0, 0] if in_vmem else total + seg_ref[0, s]
    start_ref[seg_count] = total


def inverse_order(order_ref, residue_ref, seg_count, in_vmem=False):
    for r in range(seg_count):
        residue_ref[order_ref[:, r : r + 1][0, 0] if in_vmem else order_ref[0, r]] = jnp.int32(r)


def first_slot(start_ref, residue_ref, seg_count, m, side):
    seg_here = lax.axis_index("seg")
    core, chip = seg_here % 2, seg_here // 2
    start = start_ref[chip * 2 + (core ^ side)]
    residue = residue_ref[(chip ^ m) * 2 + core]
    return start, (residue - start % seg_count + seg_count) % seg_count


def arrange_strain(side, src_ref, psd_ref, spectra_ref, start_ref, residue_ref, seg_count):
    slots, tiles = src_ref.shape[0], src_ref.shape[1]
    pair_slots = slots // seg_count
    psd = psd_ref[...]
    both = jnp.concatenate([psd, psd], axis=0)
    for m in range(seg_count // 2):
        _, first = first_slot(start_ref, residue_ref, seg_count, m, side)
        for j in range(pair_slots):
            row = (m * 2 + side) * pair_slots + j
            spectra_ref[pl.ds(row, tiles, stride=slots + 1), :] = src_ref[first + j * seg_count].astype(jnp.float32) * both


def chunk_masks(group):
    shape = (group.chunks, LANES)
    lanes = lax.broadcasted_iota(jnp.int32, shape, 1)
    starts = lax.broadcasted_iota(jnp.int32, shape, 0) * CHUNK
    for t in range(group.count):
        low = high = jnp.full(shape, CHUNK, jnp.int32)
        past = [group.edge_rows(t, p, shape) - starts for p in range(1, group.bins)]
        here = [(q >= 0) & (q < CHUNK) for q in past]
        for q, inside in zip(past, here):
            high = jnp.where(inside, q, high)
        for q, inside in zip(reversed(past), reversed(here)):
            low = jnp.where(inside, q, low)
        group.mask[t, 0] = jnp.where(lanes < low, 1.0, 0.0)
        group.mask[t, 1] = jnp.where(lanes >= high, 1.0, 0.0)
        group.mask[t, 2] = jnp.where(high < CHUNK, 1.0, 0.0)


def sigma_rows(group, t, psd_ref):
    bins = group.bins
    tmpl = group.tmpl[t]
    half = tmpl.shape[0] // 2
    power = (tmpl[:half] * tmpl[:half] + tmpl[half:] * tmpl[half:]) * psd_ref[...]
    shape = power.shape
    ids = lax.broadcasted_iota(jnp.int32, shape, 0) // 2 * LANES + lax.broadcasted_iota(jnp.int32, shape, 1)
    below = [ids < group.edge_rows(t, p, shape) for p in range(1, bins)]
    parts = []
    for p in range(bins):
        if p == 0:
            member = below[0]
        elif p == bins - 1:
            member = ~below[p - 1]
        else:
            member = below[p] & ~below[p - 1]
        part = jnp.where(member, power, 0.0)
        part = functools.reduce(jnp.add, [part[i : i + 8] for i in range(0, half, 8)])
        part = part + pltpu.roll(part, 4, 0)
        part = part + pltpu.roll(part, 2, 0)
        parts.append(jnp.broadcast_to(jnp.sum(part, axis=1, keepdims=True), (8, LANES)))
    total = functools.reduce(jnp.add, parts)
    for p in range(bins):
        group.inv[t, p] = 1.0 / parts[p]
        group.frac[t, p] = parts[p] / total
    group.inv[t, bins] = 1.0 / total


class Group:
    def __init__(self, tmpl_ref, first, splat_ref, series_ref, inv_ref, frac_ref, mask_ref=None):
        self.tmpl, self.first, self.splat = tmpl_ref, first, splat_ref
        self.series, self.inv, self.frac, self.mask = series_ref, inv_ref, frac_ref, mask_ref
        self.count, self.rows, self.bins = series_ref.shape[0], series_ref.shape[2], splat_ref.shape[0] - 1
        self.chunks = series_ref.shape[1] - (self.bins - 1)

    def edge_rows(self, t, p, shape):
        return jnp.broadcast_to(self.splat[p, pl.ds(self.first + t, 1), :], shape)

    def edge(self, t, p):
        return self.splat[p, pl.ds(self.first + t, 1), :][0, 0]

    def chunk_of(self, t, p):
        return lax.shift_right_logical(self.edge(t, p), CHUNK.bit_length() - 1)

    def inside(self, t, p):
        return self.chunk_of(t, p) == self.chunk_of(t, p + 1)


def product(group, spectra_ref, t, chunk):
    slots = group.rows // 2

    def rows_of(ref, start, step, count):
        parts = [ref[pl.ds(start + d * step, count), :] for d in range(2)]
        return jnp.concatenate([jnp.broadcast_to(part, (slots, LANES)) for part in parts], axis=0)

    tiles = (chunk, group.chunks + chunk)
    tmpl_re, tmpl_im = (rows_of(group.tmpl.at[t], tile * 2, 1, 1) for tile in tiles)
    strain_re, strain_im = (rows_of(spectra_ref, tile * 2 * (slots + 1), slots + 1, slots) for tile in tiles)
    prod_re = tmpl_re * strain_re + tmpl_im * strain_im
    prod_im = tmpl_re * strain_im - tmpl_im * strain_re
    return jnp.concatenate([prod_re, prod_im], axis=1).astype(jnp.bfloat16)


def masked(prod, member):
    member = jnp.broadcast_to(member, (16, LANES)).astype(jnp.bfloat16)
    member = jnp.concatenate([member] * (prod.shape[0] // 16), axis=0)
    return prod * jnp.concatenate([member, member], axis=1)


def add_up(group, spectra_ref, psd_ref, dft_ref, beside=()):
    chunk_masks(group)
    for t in range(group.count):
        sigma_rows(group, t, psd_ref)
    rows = group.rows
    beside = dict(beside)
    running = [jnp.zeros((rows, 2 * TIME_LAGS), jnp.float32) for _ in range(group.count)]
    for c in range(group.chunks):
        stack = []
        for t in range(group.count):
            prod = product(group, spectra_ref, t, c)
            stack.append(masked(prod, group.mask[t, 0, c : c + 1, :]))
            stack.append(masked(prod, group.mask[t, 1, c : c + 1, :]))
        got = jnp.dot(jnp.concatenate(stack, axis=0), dft_ref[c], preferred_element_type=jnp.float32)
        for t in range(group.count):
            ended = running[t] + got[2 * t * rows : (2 * t + 1) * rows]
            group.series[t, c] = ended
            cross = jnp.broadcast_to(group.mask[t, 2, c : c + 1, :], (rows, LANES)) > 0.5
            running[t] = jnp.where(cross, got[(2 * t + 1) * rows : (2 * t + 2) * rows], ended)
        for write in beside.get(c, ()):
            write()
    for t in range(group.count):
        group.series[t, group.chunks] = running[t]

    chunk_of = [[group.chunk_of(t, p) for p in range(1, group.bins)] for t in range(group.count)]
    pairs = [pair for row in chunk_of for pair in zip(row, row[1:])]
    any_inside = functools.reduce(jnp.logical_or, [a == b for a, b in pairs])

    @pl.when(any_inside)
    def _():
        def one(i, _):
            t, p = i // (group.bins - 2), i % (group.bins - 2) + 1

            @pl.when(group.inside(t, p))
            def _():
                c = group.chunk_of(t, p)
                ids = lax.broadcasted_iota(jnp.int32, (1, LANES), 1) + c * CHUNK
                member = jnp.where((ids >= group.edge(t, p)) & (ids < group.edge(t, p + 1)), 1.0, 0.0)
                prod = masked(product(group, spectra_ref, t, c), member)
                group.series[t, group.chunks + p] = jnp.dot(prod, dft_ref[c], preferred_element_type=jnp.float32)

            return 0

        lax.fori_loop(0, len(pairs), one, 0)


def test_values(group, t, out_ref):
    slots, bins = group.rows // 2, group.bins
    row = group.first + t

    def spread(ref, p):
        return jnp.concatenate(
            [jnp.broadcast_to(ref[t, p, d : d + 1, :], (slots, LANES)) for d in range(2)], axis=0
        )

    chunk_of = [group.chunk_of(t, p) for p in range(1, bins)]
    series = [group.series[t, chunk_of[0]]]
    for p in range(1, bins - 1):
        at = jnp.where(chunk_of[p - 1] == chunk_of[p], group.chunks + p, chunk_of[p])
        series.append(group.series[t, at])
    series.append(group.series[t, group.chunks])
    whole = functools.reduce(jnp.add, series)
    chi = jnp.zeros((group.rows, LANES), jnp.float32)
    for p in range(bins):
        dev = series[p] - spread(group.frac, p) * whole
        chi = chi + dev * dev * spread(group.inv, p)
    chi = jnp.sum(chi[:slots] + chi[slots:], axis=1, keepdims=True) / (TIME_LAGS * 2.0 * 2 * (bins - 1))
    power = whole * whole * spread(group.inv, bins)
    power = power[:slots] + power[slots:]
    power = power + pltpu.roll(power, TIME_LAGS, 1)
    peak = jnp.sqrt(jnp.max(power, axis=1, keepdims=True))
    out_ids = lax.broadcasted_iota(jnp.int32, (slots, LANES), 1)
    out = jnp.where(out_ids == row, peak, out_ref[...])
    out_ref[...] = jnp.where(out_ids == row + group.splat.shape[1], chi, out)


def values_of(group, out_ref):
    return [functools.partial(test_values, group, t, out_ref) for t in range(group.count)]


def own_kernel(
    seg_count,
    other_ref, own_any, tmpl_any, psd_any, dft_any, order_any, seg_any, edge_any,
    spectra_ref, dft_ref, psd_ref, splat_ref, order_lanes_ref, seg_lanes_ref, series_ref, inv_ref, frac_ref,
    own_ref, tmpl_ref, lanes_ref, order_ref, seg_ref, start_ref, residue_ref, mask_ref, sems,
):
    pairs = [
        (order_any, order_ref), (seg_any, seg_ref), (psd_any, psd_ref), (edge_any, lanes_ref), (tmpl_any, tmpl_ref),
        (own_any, own_ref), (dft_any, dft_ref), (order_any, order_lanes_ref), (seg_any, seg_lanes_ref),
    ]
    copies = [pltpu.make_async_copy(src, dst, sems.at[i]) for i, (src, dst) in enumerate(pairs)]
    for copy in copies:
        copy.start()
    for copy in copies[:4]:
        copy.wait()
    for p in range(splat_ref.shape[0]):
        splat_ref[p] = jnp.broadcast_to(lanes_ref[:, p : p + 1], splat_ref.shape[1:])
    seg_starts(seg_ref, start_ref, seg_count)
    inverse_order(order_ref, residue_ref, seg_count)
    arrange_strain(1, other_ref, psd_ref, spectra_ref, start_ref, residue_ref, seg_count)
    copies[4].wait()
    copies[5].wait()
    arrange_strain(0, own_ref, psd_ref, spectra_ref, start_ref, residue_ref, seg_count)
    for copy in copies[6:]:
        copy.wait()
    first = lax.axis_index("bank") * tmpl_ref.shape[0]
    group = Group(tmpl_ref, first, splat_ref, series_ref, inv_ref, frac_ref, mask_ref)
    add_up(group, spectra_ref, psd_ref, dft_ref)


def next_kernel(
    tmpl_ref, spectra_ref, dft_ref, psd_ref, splat_ref, old_series_ref, old_inv_ref, old_frac_ref,
    out_ref, series_ref, inv_ref, frac_ref, mask_ref,
):
    bank, count = lax.axis_index("bank"), tmpl_ref.shape[0]
    out_ref[...] = jnp.zeros_like(out_ref)
    old = Group(None, bank * count, splat_ref, old_series_ref, old_inv_ref, old_frac_ref)
    group = Group(tmpl_ref, (bank ^ (1 + core_here())) * count, splat_ref, series_ref, inv_ref, frac_ref, mask_ref)
    beside = {4 * n + 3: [write] for n, write in enumerate(values_of(old, out_ref))}
    add_up(group, spectra_ref, psd_ref, dft_ref, beside)
    for write in values_of(group, out_ref):
        write()


def mid_kernel(source, old_source, tmpl_ref, spectra_ref, dft_ref, psd_ref, splat_ref, old, out_ref, sums, mask_ref):
    bank, count = lax.axis_index("bank"), tmpl_ref.shape[0]
    group = Group(tmpl_ref, (bank ^ source()) * count, splat_ref, *sums, mask_ref)
    out_ref[...] = old[0][...]
    beside = {}
    if old_source is not None:
        writes = values_of(Group(None, (bank ^ old_source()) * count, splat_ref, *old[1:]), out_ref)
        beside = {4 * n + 3: [write] for n, write in enumerate(writes)}
    add_up(group, spectra_ref, psd_ref, dft_ref, beside)


def last_kernel(
    seg_count, sources, tmpl_ref, spectra_ref, dft_ref, psd_ref, splat_ref, order_ref, seg_ref, old_sums, part_ref,
    out_refs, sums, mask_ref, all_ref, placed_ref, start_ref, residue_ref, place_ref,
):
    pair_slots = all_ref.shape[0] // seg_count
    seg_here = lax.axis_index("seg")
    core, chip = seg_here % 2, seg_here // 2

    def place():
        seg_starts(seg_ref, start_ref, seg_count, in_vmem=True)
        inverse_order(order_ref, residue_ref, seg_count, in_vmem=True)
        for m in range(seg_count // 2):
            for source in range(2):
                start, first = first_slot(start_ref, residue_ref, seg_count, m, core ^ source)
                stop = start_ref[chip * 2 + source + 1]
                live = (stop - start - first + seg_count - 1) // seg_count
                place_ref[4 * m + 2 * source] = (start + first) // seg_count
                place_ref[4 * m + 2 * source + 1] = live

    bank, count = lax.axis_index("bank"), tmpl_ref.shape[0]
    all_ref[...] = part_ref[...]
    placed_ref[...] = jnp.zeros_like(placed_ref)
    old = Group(None, (bank ^ sources[0]()) * count, splat_ref, *old_sums)
    group = Group(tmpl_ref, (bank ^ sources[1]()) * count, splat_ref, *sums, mask_ref)
    writes = values_of(old, all_ref)
    add_up(group, spectra_ref, psd_ref, dft_ref, {3: writes[:1], 6: writes[1:2], 8: [place], 9: writes[2:]})
    for write in values_of(group, all_ref):
        write()
    ids = lax.broadcasted_iota(jnp.int32, (pair_slots, LANES), 0)
    for m in range(seg_count // 2):
        for source in range(2):
            values = all_ref[pl.ds((m * 2 + (core ^ source)) * pair_slots, pair_slots), :]
            values = jnp.where(ids < place_ref[4 * m + 2 * source + 1], values, 0.0)
            placed_ref[m, pl.ds(place_ref[4 * m + 2 * source], pair_slots), :] = values
        out_refs[m][...] = placed_ref[m, :BLK_DEV]


def add_kernel(part_refs, peak_ref, chi_ref):
    tmpl_total = peak_ref.shape[1]
    rows = functools.reduce(jnp.add, [ref[...] for ref in part_refs])
    peak_ref[...] = rows[:, :tmpl_total]
    chi_ref[...] = rows[:, tmpl_total : 2 * tmpl_total]


def swap(x, axis, step):
    return lax.ppermute(x, axis, [(i, i ^ step) for i in range(lax.axis_size(axis))])


def body(strain, templates, inv_psd, seg_blocks, dest_order, bin_edges):
    seg_count, bank_count = lax.axis_size("seg"), lax.axis_size("bank")
    chip_count = seg_count // 2
    slots, detectors, width = strain.shape
    freq_count = width // 2
    tmpl_total, bins = bin_edges.shape[0], bin_edges.shape[1] - 1
    tmpl_count = templates.shape[0]
    rows = detectors * slots
    tiles = detectors * width // LANES
    f32, i32 = jnp.float32, jnp.int32
    dft = jnp.asarray(dft_chunks(freq_count))
    psd = tile_rows(inv_psd)

    other = tile_rows(swap(strain, "seg", 1))
    far = [tile_rows(swap(templates, "bank", s)) for s in range(3, bank_count)]
    near = [(b * seg_count + s, (b ^ (1 + s % 2)) * seg_count + s) for b in range(bank_count) for s in range(seg_count)]
    near = lax.ppermute(templates, ("bank", "seg"), near)

    def shape(*dims, dtype=f32):
        return jax.ShapeDtypeStruct(dims, dtype)

    chunks = freq_count // CHUNK
    sums = [(tmpl_count, chunks + bins - 1, rows, 2 * TIME_LAGS)] + [(tmpl_count, bins + 1, 8, LANES)] * 2
    sum_shapes = tuple(shape(*dims) for dims in sums)
    mask = pltpu.VMEM((tmpl_count, 3, chunks, LANES), f32)
    tables = [pltpu.SMEM((seg_count + 1,), i32), pltpu.SMEM((seg_count,), i32)]

    def call(kernel, name, flops, bytes_accessed=4 * 10**6, **kwargs):
        return pl.pallas_call(
            kernel,
            name=name,
            cost_estimate=pl.CostEstimate(flops=flops, bytes_accessed=bytes_accessed, transcendentals=0),
            compiler_params=pltpu.CompilerParams(vmem_limit_bytes=40 * 1024 * 1024),
            **kwargs,
        )

    hbm = pl.BlockSpec(memory_space=pltpu.HBM)

    def in_hbm(*arrays):
        return [pltpu.with_memory_space_constraint(x, pltpu.HBM) for x in arrays]

    splat_shape = shape(bins + 1, tmpl_total, LANES, dtype=i32)
    spectra, dft_held, psd_held, splat, order_held, seg_held, *own_sums = call(
        functools.partial(own_kernel, seg_count),
        "own_templates",
        10**9,
        out_shape=(shape((slots + 1) * tiles, LANES), shape(*dft.shape, dtype=dft.dtype), shape(*psd.shape), splat_shape)
        + (shape(*dest_order.shape, dtype=i32), shape(*seg_blocks.shape, dtype=i32))
        + sum_shapes,
        in_specs=[VMEM] + [hbm] * 7,
        out_specs=(VMEM,) * 9,
        scratch_shapes=[
            pltpu.VMEM((slots, tiles, LANES), strain.dtype),
            pltpu.VMEM((tmpl_count, tiles, LANES), f32),
            pltpu.VMEM(bin_edges.shape, i32),
            pltpu.SMEM(dest_order.shape, i32),
            pltpu.SMEM(seg_blocks.shape, i32),
        ]
        + tables
        + [mask, pltpu.SemaphoreType.DMA((9,))],
    )(other, *in_hbm(tile_rows(strain), tile_rows(templates), psd, dft, dest_order, seg_blocks, bin_edges))

    near, spectra = lax.optimization_barrier((near, spectra))
    held = (spectra, dft_held, psd_held, splat)
    out = call(
        next_kernel,
        "next_templates",
        1,
        1,
        out_shape=shape(slots, LANES),
        in_specs=[VMEM] * 8,
        out_specs=VMEM,
        scratch_shapes=[pltpu.VMEM(dims, f32) for dims in sums] + [mask],
    )(tile_rows(near), *held, *own_sums)

    sources = [functools.partial(int, s) for s in range(3, bank_count)] + [lambda: 2 - core_here()]
    remote = far + [tile_rows(swap(near, "seg", 1))]
    old = [out]
    for n, tmpl in enumerate(remote[:-1]):

        def mid(*refs, n=n, count=len(old)):
            ins, olds, (out_ref, *sums_out, mask_ref) = refs[:5], refs[5 : 5 + count], refs[5 + count :]
            mid_kernel(sources[n], sources[n - 1] if n else None, *ins, olds, out_ref, sums_out, mask_ref)

        old = call(
            mid,
            "mid_templates",
            1,
            1,
            out_shape=(shape(slots, LANES),) + sum_shapes,
            in_specs=[VMEM] * (5 + len(old)),
            out_specs=(VMEM,) * 4,
            scratch_shapes=[mask],
        )(tmpl, *held, *old)

    def last(*refs):
        ins, part_ref, sums_in, refs = refs[:7], refs[7], refs[8:11], refs[11:]
        outs, refs = refs[:chip_count], refs[chip_count:]
        last_kernel(seg_count, sources[-2:], *ins, sums_in, part_ref, outs, refs[:3], *refs[3:])

    parts = call(
        last,
        "last_templates",
        10**9,
        out_shape=(shape(BLK_DEV, LANES),) * chip_count,
        in_specs=[VMEM] * 11,
        out_specs=(VMEM,) * chip_count,
        scratch_shapes=[pltpu.VMEM(dims, f32) for dims in sums]
        + [mask]
        + [pltpu.VMEM((slots, LANES), f32), pltpu.VMEM((chip_count, BLK_DEV + 8, LANES), f32)]
        + tables
        + [pltpu.SMEM((4 * chip_count,), i32)],
    )(remote[-1], *held, order_held, seg_held, *old)

    got = [swap(parts[m], "seg", 2 * m) for m in reversed(range(1, chip_count))] + [parts[0]]
    return call(
        lambda *refs: add_kernel(refs[:chip_count], *refs[chip_count:]),
        "add_rows",
        10**5,
        out_shape=(shape(BLK_DEV, tmpl_total),) * 2,
        in_specs=[VMEM] * chip_count,
        out_specs=(VMEM, VMEM),
    )(*got)


def solution(mesh):
    return jax.shard_map(
        body,
        mesh=mesh,
        in_specs=(
            P(("bank", "seg"), None, None),
            P("bank", None, None),
            P(),
            P("bank", None),
            P("bank", None),
            P(),
        ),
        out_specs=(P(("bank", "seg"), None), P(("bank", "seg"), None)),
        check_vma=False,
    )
```

```python
import functools

import jax
import jax.numpy as jnp
import ml_dtypes
import numpy as np
from jax import lax
from jax.experimental import pallas as pl
from jax.experimental.pallas import tpu as pltpu
from jax.sharding import PartitionSpec as P

TIME_LAGS = 64
BLK_DEV = 16
CHUNK = 128
LANES = 128
VMEM = pl.BlockSpec(memory_space=pltpu.VMEM)
SMEM = pl.BlockSpec(memory_space=pltpu.SMEM)


def dft_chunks(freq_count):
    turns = np.arange(freq_count)[:, None] * np.arange(TIME_LAGS)[None, :] % (2 * freq_count)
    angle = turns * (np.pi / freq_count)
    cosine, sine = np.cos(angle), np.sin(angle)
    upper = np.concatenate([cosine, sine], axis=1).reshape(-1, CHUNK, 2 * TIME_LAGS)
    lower = np.concatenate([-sine, cosine], axis=1).reshape(-1, CHUNK, 2 * TIME_LAGS)
    return np.concatenate([upper, lower], axis=1).astype(np.float32).astype(ml_dtypes.bfloat16)


def tile_rows(x):
    lead, (detectors, width) = x.shape[:-2], x.shape[-2:]
    tiles = jnp.swapaxes(x.reshape(lead + (detectors, width // LANES, LANES)), -3, -2)
    return tiles.reshape(lead + (detectors * width // LANES, LANES))


def core_here():
    return lax.axis_index("seg") % 2


def seg_starts(seg_ref, start_ref, seg_count):
    total = jnp.int32(0)
    for s in range(seg_count):
        start_ref[s] = total
        total = total + seg_ref[:, s : s + 1][0, 0]
    start_ref[seg_count] = total


def inverse_order(order_ref, residue_ref, seg_count):
    for r in range(seg_count):
        residue_ref[order_ref[:, r : r + 1][0, 0]] = jnp.int32(r)


def first_slot(start_ref, residue_ref, seg_count, m, side):
    seg_here = lax.axis_index("seg")
    core, chip = seg_here % 2, seg_here // 2
    start = start_ref[chip * 2 + (core ^ side)]
    residue = residue_ref[(chip ^ m) * 2 + core]
    return start, (residue - start % seg_count + seg_count) % seg_count


def arrange_strain(side, src_ref, psd_ref, spectra_ref, start_ref, residue_ref, seg_count):
    slots, tiles = src_ref.shape[0], src_ref.shape[1]
    pair_slots = slots // seg_count
    psd = psd_ref[...]
    both = jnp.concatenate([psd, psd], axis=0)
    for m in range(seg_count // 2):
        _, first = first_slot(start_ref, residue_ref, seg_count, m, side)
        for j in range(pair_slots):
            row = (m * 2 + side) * pair_slots + j
            spectra_ref[pl.ds(row, tiles, stride=slots + 1), :] = src_ref[first + j * seg_count].astype(jnp.float32) * both


def chunk_masks(group):
    shape = (group.chunks, LANES)
    lanes = lax.broadcasted_iota(jnp.int32, shape, 1)
    starts = lax.broadcasted_iota(jnp.int32, shape, 0) * CHUNK
    for t in range(group.count):
        low = high = jnp.full(shape, CHUNK, jnp.int32)
        past = [group.edge_rows(t, p, shape) - starts for p in range(1, group.bins)]
        here = [(q >= 0) & (q < CHUNK) for q in past]
        for q, inside in zip(past, here):
            high = jnp.where(inside, q, high)
        for q, inside in zip(reversed(past), reversed(here)):
            low = jnp.where(inside, q, low)
        group.mask[t, 0] = jnp.where(lanes < low, 1.0, 0.0)
        group.mask[t, 1] = jnp.where(lanes >= high, 1.0, 0.0)
        group.mask[t, 2] = jnp.where(high < CHUNK, 1.0, 0.0)


def sigma_rows(group, t, psd_ref):
    bins = group.bins
    tmpl = group.tmpl[t]
    half = tmpl.shape[0] // 2
    power = (tmpl[:half] * tmpl[:half] + tmpl[half:] * tmpl[half:]) * psd_ref[...]
    shape = power.shape
    ids = lax.broadcasted_iota(jnp.int32, shape, 0) // 2 * LANES + lax.broadcasted_iota(jnp.int32, shape, 1)
    below = [ids < group.edge_rows(t, p, shape) for p in range(1, bins)]
    parts = []
    for p in range(bins):
        if p == 0:
            member = below[0]
        elif p == bins - 1:
            member = ~below[p - 1]
        else:
            member = below[p] & ~below[p - 1]
        part = jnp.where(member, power, 0.0)
        part = functools.reduce(jnp.add, [part[i : i + 8] for i in range(0, half, 8)])
        part = part + pltpu.roll(part, 4, 0)
        part = part + pltpu.roll(part, 2, 0)
        parts.append(jnp.broadcast_to(jnp.sum(part, axis=1, keepdims=True), (8, LANES)))
    total = functools.reduce(jnp.add, parts)
    for p in range(bins):
        group.inv[t, p] = 1.0 / parts[p]
        group.frac[t, p] = parts[p] / total
    group.inv[t, bins] = 1.0 / total


class Group:
    def __init__(self, tmpl_ref, first, splat_ref, series_ref, inv_ref, frac_ref, mask_ref=None):
        self.tmpl, self.first, self.splat = tmpl_ref, first, splat_ref
        self.series, self.inv, self.frac, self.mask = series_ref, inv_ref, frac_ref, mask_ref
        self.count, self.rows, self.bins = series_ref.shape[0], series_ref.shape[2], splat_ref.shape[0] - 1
        self.chunks = series_ref.shape[1] - (self.bins - 1)

    def edge_rows(self, t, p, shape):
        return jnp.broadcast_to(self.splat[p, pl.ds(self.first + t, 1), :], shape)

    def edge(self, t, p):
        return self.splat[p, pl.ds(self.first + t, 1), :][0, 0]

    def chunk_of(self, t, p):
        return lax.shift_right_logical(self.edge(t, p), CHUNK.bit_length() - 1)

    def inside(self, t, p):
        return self.chunk_of(t, p) == self.chunk_of(t, p + 1)


def product(group, spectra_ref, t, chunk):
    slots = group.rows // 2

    def rows_of(ref, start, step, count):
        parts = [ref[pl.ds(start + d * step, count), :] for d in range(2)]
        return jnp.concatenate([jnp.broadcast_to(part, (slots, LANES)) for part in parts], axis=0)

    tiles = (chunk, group.chunks + chunk)
    tmpl_re, tmpl_im = (rows_of(group.tmpl.at[t], tile * 2, 1, 1) for tile in tiles)
    strain_re, strain_im = (rows_of(spectra_ref, tile * 2 * (slots + 1), slots + 1, slots) for tile in tiles)
    prod_re = tmpl_re * strain_re + tmpl_im * strain_im
    prod_im = tmpl_re * strain_im - tmpl_im * strain_re
    return jnp.concatenate([prod_re, prod_im], axis=1).astype(jnp.bfloat16)


def masked(prod, member):
    member = jnp.broadcast_to(member, (16, LANES)).astype(jnp.bfloat16)
    member = jnp.concatenate([member] * (prod.shape[0] // 16), axis=0)
    return prod * jnp.concatenate([member, member], axis=1)


def add_up(group, spectra_ref, psd_ref, dft_ref, beside=()):
    chunk_masks(group)
    for t in range(group.count):
        sigma_rows(group, t, psd_ref)
    rows = group.rows
    beside = dict(beside)
    running = [jnp.zeros((rows, 2 * TIME_LAGS), jnp.float32) for _ in range(group.count)]
    for c in range(group.chunks):
        stack = []
        for t in range(group.count):
            prod = product(group, spectra_ref, t, c)
            stack.append(masked(prod, group.mask[t, 0, c : c + 1, :]))
            stack.append(masked(prod, group.mask[t, 1, c : c + 1, :]))
        got = jnp.dot(jnp.concatenate(stack, axis=0), dft_ref[c], preferred_element_type=jnp.float32)
        for t in range(group.count):
            ended = running[t] + got[2 * t * rows : (2 * t + 1) * rows]
            group.series[t, c] = ended
            cross = jnp.broadcast_to(group.mask[t, 2, c : c + 1, :], (rows, LANES)) > 0.5
            running[t] = jnp.where(cross, got[(2 * t + 1) * rows : (2 * t + 2) * rows], ended)
        for write in beside.get(c, ()):
            write()
    for t in range(group.count):
        group.series[t, group.chunks] = running[t]

    chunk_of = [[group.chunk_of(t, p) for p in range(1, group.bins)] for t in range(group.count)]
    pairs = [pair for row in chunk_of for pair in zip(row, row[1:])]
    any_inside = functools.reduce(jnp.logical_or, [a == b for a, b in pairs])

    @pl.when(any_inside)
    def _():
        def one(i, _):
            t, p = i // (group.bins - 2), i % (group.bins - 2) + 1

            @pl.when(group.inside(t, p))
            def _():
                c = group.chunk_of(t, p)
                ids = lax.broadcasted_iota(jnp.int32, (1, LANES), 1) + c * CHUNK
                member = jnp.where((ids >= group.edge(t, p)) & (ids < group.edge(t, p + 1)), 1.0, 0.0)
                prod = masked(product(group, spectra_ref, t, c), member)
                group.series[t, group.chunks + p] = jnp.dot(prod, dft_ref[c], preferred_element_type=jnp.float32)

            return 0

        lax.fori_loop(0, len(pairs), one, 0)


def test_values(group, t, out_ref):
    slots, bins = group.rows // 2, group.bins
    row = group.first + t

    def spread(ref, p):
        return jnp.concatenate(
            [jnp.broadcast_to(ref[t, p, d : d + 1, :], (slots, LANES)) for d in range(2)], axis=0
        )

    chunk_of = [group.chunk_of(t, p) for p in range(1, bins)]
    series = [group.series[t, chunk_of[0]]]
    for p in range(1, bins - 1):
        at = jnp.where(chunk_of[p - 1] == chunk_of[p], group.chunks + p, chunk_of[p])
        series.append(group.series[t, at])
    series.append(group.series[t, group.chunks])
    whole = functools.reduce(jnp.add, series)
    chi = jnp.zeros((group.rows, LANES), jnp.float32)
    for p in range(bins):
        dev = series[p] - spread(group.frac, p) * whole
        chi = chi + dev * dev * spread(group.inv, p)
    chi = jnp.sum(chi[:slots] + chi[slots:], axis=1, keepdims=True) / (TIME_LAGS * 2.0 * 2 * (bins - 1))
    power = whole * whole * spread(group.inv, bins)
    power = power[:slots] + power[slots:]
    power = power + pltpu.roll(power, TIME_LAGS, 1)
    peak = jnp.sqrt(jnp.max(power, axis=1, keepdims=True))
    out_ids = lax.broadcasted_iota(jnp.int32, (slots, LANES), 1)
    out = jnp.where(out_ids == row, peak, out_ref[...])
    out_ref[...] = jnp.where(out_ids == row + group.splat.shape[1], chi, out)


def values_of(group, out_ref):
    return [functools.partial(test_values, group, t, out_ref) for t in range(group.count)]


def begin_kernel(out_ref):
    out_ref[...] = jnp.zeros_like(out_ref)


def own_kernel(
    seg_count,
    _, other_ref, own_ref, tmpl_ref, psd_ref, dft_ref, order_ref, seg_ref, edge_ref,
    spectra_ref, splat_ref, out_ref,
    start_ref, residue_ref, mask_ref, series_ref, inv_ref, frac_ref,
):
    for p in range(splat_ref.shape[0]):
        splat_ref[p] = jnp.broadcast_to(edge_ref[:, p : p + 1], splat_ref.shape[1:])
    seg_starts(seg_ref, start_ref, seg_count)
    inverse_order(order_ref, residue_ref, seg_count)
    arrange_strain(0, own_ref, psd_ref, spectra_ref, start_ref, residue_ref, seg_count)
    arrange_strain(1, other_ref, psd_ref, spectra_ref, start_ref, residue_ref, seg_count)
    first = lax.axis_index("bank") * tmpl_ref.shape[0]
    group = Group(tmpl_ref, first, splat_ref, series_ref, inv_ref, frac_ref, mask_ref)
    add_up(group, spectra_ref, psd_ref, dft_ref)
    out_ref[...] = jnp.zeros_like(out_ref)
    for write in values_of(group, out_ref):
        write()


def mid_kernel(source, old_source, tmpl_ref, spectra_ref, dft_ref, psd_ref, splat_ref, old, sums, out_ref, mask_ref):
    bank, count = lax.axis_index("bank"), tmpl_ref.shape[0]
    group = Group(tmpl_ref, (bank ^ source()) * count, splat_ref, *sums, mask_ref)
    beside = {}
    if old:
        out_ref[...] = old[3][...]
        writes = values_of(Group(None, (bank ^ old_source()) * count, splat_ref, *old[:3]), out_ref)
        beside = {4 * n + 3: [write] for n, write in enumerate(writes)}
    add_up(group, spectra_ref, psd_ref, dft_ref, beside)


def last_kernel(
    seg_count, sources, tmpl_ref, spectra_ref, dft_ref, psd_ref, splat_ref, order_ref, seg_ref, old_sums, part_ref,
    out_refs, sums, mask_ref, all_ref, placed_ref, start_ref, residue_ref, place_ref,
):
    pair_slots = all_ref.shape[0] // seg_count
    seg_here = lax.axis_index("seg")
    core, chip = seg_here % 2, seg_here // 2

    def place():
        seg_starts(seg_ref, start_ref, seg_count)
        inverse_order(order_ref, residue_ref, seg_count)
        for m in range(seg_count // 2):
            for source in range(2):
                start, first = first_slot(start_ref, residue_ref, seg_count, m, core ^ source)
                stop = start_ref[chip * 2 + source + 1]
                live = (stop - start - first + seg_count - 1) // seg_count
                place_ref[4 * m + 2 * source] = (start + first) // seg_count
                place_ref[4 * m + 2 * source + 1] = live

    bank, count = lax.axis_index("bank"), tmpl_ref.shape[0]
    all_ref[...] = part_ref[...]
    placed_ref[...] = jnp.zeros_like(placed_ref)
    old = Group(None, (bank ^ sources[0]()) * count, splat_ref, *old_sums)
    group = Group(tmpl_ref, (bank ^ sources[1]()) * count, splat_ref, *sums, mask_ref)
    writes = values_of(old, all_ref)
    add_up(group, spectra_ref, psd_ref, dft_ref, {3: writes[:1], 6: writes[1:2], 8: [place], 9: writes[2:]})
    for write in values_of(group, all_ref):
        write()
    ids = lax.broadcasted_iota(jnp.int32, (pair_slots, LANES), 0)
    for m in range(seg_count // 2):
        for source in range(2):
            values = all_ref[pl.ds((m * 2 + (core ^ source)) * pair_slots, pair_slots), :]
            values = jnp.where(ids < place_ref[4 * m + 2 * source + 1], values, 0.0)
            placed_ref[m, pl.ds(place_ref[4 * m + 2 * source], pair_slots), :] = values
        out_refs[m][...] = placed_ref[m, :BLK_DEV]


def add_kernel(part_refs, peak_ref, chi_ref):
    tmpl_total = peak_ref.shape[1]
    rows = functools.reduce(jnp.add, [ref[...] for ref in part_refs])
    peak_ref[...] = rows[:, :tmpl_total]
    chi_ref[...] = rows[:, tmpl_total : 2 * tmpl_total]


def swap(x, axis, step):
    return lax.ppermute(x, axis, [(i, i ^ step) for i in range(lax.axis_size(axis))])


def body(strain, templates, inv_psd, seg_blocks, dest_order, bin_edges):
    seg_count, bank_count = lax.axis_size("seg"), lax.axis_size("bank")
    chip_count = seg_count // 2
    slots, detectors, width = strain.shape
    freq_count = width // 2
    tmpl_total, bins = bin_edges.shape[0], bin_edges.shape[1] - 1
    tmpl_count = templates.shape[0]
    rows = detectors * slots
    tiles = detectors * width // LANES
    f32, i32 = jnp.float32, jnp.int32
    dft = jnp.asarray(dft_chunks(freq_count))
    psd = tile_rows(inv_psd)

    def shape(*dims, dtype=f32):
        return jax.ShapeDtypeStruct(dims, dtype)

    chunks = freq_count // CHUNK
    sums = [(tmpl_count, chunks + bins - 1, rows, 2 * TIME_LAGS)] + [(tmpl_count, bins + 1, 8, LANES)] * 2
    sum_shapes = tuple(shape(*dims) for dims in sums)
    mask = pltpu.VMEM((tmpl_count, 3, chunks, LANES), f32)
    tables = [pltpu.SMEM((seg_count + 1,), i32), pltpu.SMEM((seg_count,), i32)]

    def call(kernel, name, flops, bytes_accessed=4 * 10**6, **kwargs):
        return pl.pallas_call(
            kernel,
            name=name,
            cost_estimate=pl.CostEstimate(flops=flops, bytes_accessed=bytes_accessed, transcendentals=0),
            compiler_params=pltpu.CompilerParams(vmem_limit_bytes=40 * 1024 * 1024),
            **kwargs,
        )

    begin = call(begin_kernel, "begin", 2 * 10**9, 1, out_shape=shape(8, LANES), out_specs=VMEM)()
    other = tile_rows(swap(strain, "seg", 1))
    far = [tile_rows(swap(templates, "bank", s)) for s in range(3, bank_count)]
    near = [(b * seg_count + s, (b ^ (1 + s % 2)) * seg_count + s) for b in range(bank_count) for s in range(seg_count)]
    near = lax.ppermute(templates, ("bank", "seg"), near)

    splat_shape = shape(bins + 1, tmpl_total, LANES, dtype=i32)
    spectra, splat, out = call(
        functools.partial(own_kernel, seg_count),
        "own_templates",
        10**9,
        out_shape=(shape((slots + 1) * tiles, LANES), splat_shape, shape(slots, LANES)),
        in_specs=[VMEM] * 9,
        out_specs=(VMEM,) * 3,
        scratch_shapes=tables + [mask] + [pltpu.VMEM(dims, f32) for dims in sums],
    )(begin, other, tile_rows(strain), tile_rows(templates), psd, dft, dest_order, seg_blocks, bin_edges)

    near, spectra = lax.optimization_barrier((near, spectra))
    held = (spectra, dft, psd, splat)
    sources = [lambda: 1 + core_here(), lambda: 2 - core_here()]
    sources += [functools.partial(int, s) for s in range(3, bank_count)]
    remote = [[tile_rows(near)], [tile_rows(swap(part, "seg", 1)) for part in (near[:2], near[2:])]]
    remote += [[x] for x in far]
    old = []
    for n, parts in enumerate(remote[:-1]):

        def mid(*refs, n=n, count=len(old), split=len(parts)):
            parts, refs = refs[:split], refs[split:]
            ins, olds, (*outs, mask_ref, tmpl_ref) = refs[:4], refs[4 : 4 + count], refs[4 + count :]
            if split > 1:
                row = 0
                for ref in parts:
                    tmpl_ref[row : row + ref.shape[0]] = ref[...]
                    row += ref.shape[0]
            else:
                (tmpl_ref,) = parts
            out_ref = outs[3] if olds else None
            mid_kernel(sources[n], sources[n - 1], tmpl_ref, *ins, olds, outs[:3], out_ref, mask_ref)

        outs = sum_shapes + ((shape(slots, LANES),) if old else ())
        new = call(
            mid,
            "mid_templates" if old else "next_templates",
            1,
            1,
            out_shape=outs,
            in_specs=[VMEM] * (4 + len(parts) + len(old)),
            out_specs=(VMEM,) * len(outs),
            scratch_shapes=[mask, pltpu.VMEM((tmpl_count, tiles, LANES), f32)],
        )(*parts, *held, *old)
        old = list(new) if old else [*new, out]

    def last(*refs):
        ins, sums_in, part_ref, refs = refs[:7], refs[7:10], refs[10], refs[11:]
        outs, refs = refs[:chip_count], refs[chip_count:]
        last_kernel(seg_count, sources[-2:], *ins, sums_in, part_ref, outs, refs[:3], *refs[3:])

    parts = call(
        last,
        "last_templates",
        10**9,
        out_shape=(shape(BLK_DEV, LANES),) * chip_count,
        in_specs=[VMEM] * 11,
        out_specs=(VMEM,) * chip_count,
        scratch_shapes=[pltpu.VMEM(dims, f32) for dims in sums]
        + [mask]
        + [pltpu.VMEM((slots, LANES), f32), pltpu.VMEM((chip_count, BLK_DEV + 8, LANES), f32)]
        + tables
        + [pltpu.SMEM((4 * chip_count,), i32)],
    )(*remote[-1], *held, dest_order, seg_blocks, *old)

    got = [swap(parts[m], "seg", 2 * m) for m in reversed(range(1, chip_count))] + [parts[0]]
    return call(
        lambda *refs: add_kernel(refs[:chip_count], *refs[chip_count:]),
        "add_rows",
        10**5,
        out_shape=(shape(BLK_DEV, tmpl_total),) * 2,
        in_specs=[VMEM] * chip_count,
        out_specs=(VMEM, VMEM),
    )(*got)


def solution(mesh):
    return jax.shard_map(
        body,
        mesh=mesh,
        in_specs=(
            P(("bank", "seg"), None, None),
            P("bank", None, None),
            P(),
            P("bank", None),
            P("bank", None),
            P(),
        ),
        out_specs=(P(("bank", "seg"), None), P(("bank", "seg"), None)),
        check_vma=False,
    )
```

```python
import functools

import jax
import jax.numpy as jnp
import ml_dtypes
import numpy as np
from jax import lax
from jax.experimental import pallas as pl
from jax.experimental.pallas import tpu as pltpu
from jax.sharding import PartitionSpec as P

TIME_LAGS = 64
BLK_DEV = 16
CHUNK = 128
LANES = 128
VMEM = pl.BlockSpec(memory_space=pltpu.VMEM)
SMEM = pl.BlockSpec(memory_space=pltpu.SMEM)


def dft_chunks(freq_count):
    turns = np.arange(freq_count)[:, None] * np.arange(TIME_LAGS)[None, :] % (2 * freq_count)
    angle = turns * (np.pi / freq_count)
    cosine, sine = np.cos(angle), np.sin(angle)
    upper = np.concatenate([cosine, sine], axis=1).reshape(-1, CHUNK, 2 * TIME_LAGS)
    lower = np.concatenate([-sine, cosine], axis=1).reshape(-1, CHUNK, 2 * TIME_LAGS)
    return np.concatenate([upper, lower], axis=1).astype(np.float32).astype(ml_dtypes.bfloat16)


def tile_rows(x):
    lead, (detectors, width) = x.shape[:-2], x.shape[-2:]
    tiles = jnp.swapaxes(x.reshape(lead + (detectors, width // LANES, LANES)), -3, -2)
    return tiles.reshape(lead + (detectors * width // LANES, LANES))


def core_here():
    return lax.axis_index("seg") % 2


def seg_starts(seg_ref, start_ref, seg_count):
    total = jnp.int32(0)
    for s in range(seg_count):
        start_ref[s] = total
        total = total + seg_ref[:, s : s + 1][0, 0]
    start_ref[seg_count] = total


def inverse_order(order_ref, residue_ref, seg_count):
    for r in range(seg_count):
        residue_ref[order_ref[:, r : r + 1][0, 0]] = jnp.int32(r)


def first_slot(start_ref, residue_ref, seg_count, m, side):
    seg_here = lax.axis_index("seg")
    core, chip = seg_here % 2, seg_here // 2
    start = start_ref[chip * 2 + (core ^ side)]
    residue = residue_ref[(chip ^ m) * 2 + (core ^ (m > 0))]
    return start, (residue - start % seg_count + seg_count) % seg_count


def arrange_strain(side, src_ref, psd_ref, spectra_ref, start_ref, residue_ref, seg_count):
    slots, tiles = src_ref.shape[0], src_ref.shape[1]
    pair_slots = slots // seg_count
    psd = psd_ref[...]
    both = jnp.concatenate([psd, psd], axis=0)
    for m in range(seg_count // 2):
        _, first = first_slot(start_ref, residue_ref, seg_count, m, side)
        for j in range(pair_slots):
            row = (m * 2 + side) * pair_slots + j
            spectra_ref[pl.ds(row, tiles, stride=slots + 1), :] = src_ref[first + j * seg_count].astype(jnp.float32) * both


def chunk_masks(splat_ref, mask_ref):
    shape = mask_ref.shape[2:]
    lanes = lax.broadcasted_iota(jnp.int32, shape, 1)
    starts = lax.broadcasted_iota(jnp.int32, shape, 0) * CHUNK
    for t in range(mask_ref.shape[0]):
        low = high = jnp.full(shape, CHUNK, jnp.int32)
        past = [jnp.broadcast_to(splat_ref[p, t : t + 1, :], shape) - starts for p in range(1, splat_ref.shape[0] - 1)]
        here = [(q >= 0) & (q < CHUNK) for q in past]
        for q, inside in zip(past, here):
            high = jnp.where(inside, q, high)
        for q, inside in zip(reversed(past), reversed(here)):
            low = jnp.where(inside, q, low)
        mask_ref[t, 0] = jnp.where(lanes < low, 1.0, 0.0)
        mask_ref[t, 1] = jnp.where(lanes >= high, 1.0, 0.0)
        mask_ref[t, 2] = jnp.where(high < CHUNK, 1.0, 0.0)


def sigma_rows(group, t, psd_ref):
    bins = group.bins
    tmpl = group.tmpl[t]
    half = tmpl.shape[0] // 2
    power = (tmpl[:half] * tmpl[:half] + tmpl[half:] * tmpl[half:]) * psd_ref[...]
    shape = power.shape
    ids = lax.broadcasted_iota(jnp.int32, shape, 0) // 2 * LANES + lax.broadcasted_iota(jnp.int32, shape, 1)
    below = [ids < group.edge_rows(t, p, shape) for p in range(1, bins)]
    row_pair = lax.broadcasted_iota(jnp.int32, (8, LANES), 0) // 2
    packs = []
    for p in range(bins):
        if p == 0:
            member = below[0]
        elif p == bins - 1:
            member = ~below[p - 1]
        else:
            member = below[p] & ~below[p - 1]
        part = jnp.where(member, power, 0.0)
        part = functools.reduce(jnp.add, [part[i : i + 8] for i in range(0, half, 8)])
        part = part + pltpu.roll(part, 4, 0)
        part = part + pltpu.roll(part, 2, 0)
        if p % 4 == 0:
            packs.append(part)
        else:
            packs[-1] = jnp.where(row_pair == p % 4, part, packs[-1])
    packs = [jnp.broadcast_to(jnp.sum(x, axis=1, keepdims=True), (8, LANES)) for x in packs]
    total = functools.reduce(jnp.add, packs)
    total = total + pltpu.roll(total, 4, 0)
    total = 1.0 / (total + pltpu.roll(total, 2, 0))
    for i, pack in enumerate(packs):
        group.inv[t, 8 * i : 8 * i + 8] = 1.0 / pack
        group.frac[t, 8 * i : 8 * i + 8] = pack * total
    group.inv[t, 2 * bins : 2 * bins + 8] = total


class Group:
    def __init__(self, tmpl_ref, first, splat_ref, series_ref, inv_ref, frac_ref, mask_ref=None):
        self.tmpl, self.first, self.splat = tmpl_ref, first, splat_ref
        self.series, self.inv, self.frac, self.mask = series_ref, inv_ref, frac_ref, mask_ref
        self.count, self.rows, self.bins = series_ref.shape[0], series_ref.shape[2], splat_ref.shape[0] - 1
        self.chunks = series_ref.shape[1] - (self.bins - 1)

    def edge_rows(self, t, p, shape):
        return jnp.broadcast_to(self.splat[p, pl.ds(self.first + t, 1), :], shape)

    def mask_row(self, t, kind, c):
        return self.mask[self.first + t, kind, c : c + 1, :]

    def edge(self, t, p):
        return self.splat[p, pl.ds(self.first + t, 1), :][0, 0]

    def chunk_of(self, t, p):
        return lax.shift_right_logical(self.edge(t, p), CHUNK.bit_length() - 1)

    def inside(self, t, p):
        return self.chunk_of(t, p) == self.chunk_of(t, p + 1)


def product(group, spectra_ref, t, chunk):
    slots = group.rows // 2

    def rows_of(ref, start, step, count):
        parts = [ref[pl.ds(start + d * step, count), :] for d in range(2)]
        return jnp.concatenate([jnp.broadcast_to(part, (slots, LANES)) for part in parts], axis=0)

    tiles = (chunk, group.chunks + chunk)
    tmpl_re, tmpl_im = (rows_of(group.tmpl.at[t], tile * 2, 1, 1) for tile in tiles)
    strain_re, strain_im = (rows_of(spectra_ref, tile * 2 * (slots + 1), slots + 1, slots) for tile in tiles)
    prod_re = tmpl_re * strain_re + tmpl_im * strain_im
    prod_im = tmpl_re * strain_im - tmpl_im * strain_re
    return jnp.concatenate([prod_re, prod_im], axis=1).astype(jnp.bfloat16)


def masked(prod, member):
    member = jnp.broadcast_to(member, (16, LANES)).astype(jnp.bfloat16)
    member = jnp.concatenate([member] * (prod.shape[0] // 16), axis=0)
    return prod * jnp.concatenate([member, member], axis=1)


def add_up(group, spectra_ref, psd_ref, dft_ref, beside=()):
    for t in range(group.count):
        sigma_rows(group, t, psd_ref)
    rows = group.rows
    beside = dict(beside)
    running = [jnp.zeros((rows, 2 * TIME_LAGS), jnp.float32) for _ in range(group.count)]
    for c in range(group.chunks):
        stack = []
        for t in range(group.count):
            prod = product(group, spectra_ref, t, c)
            stack.append(masked(prod, group.mask_row(t, 0, c)))
            stack.append(masked(prod, group.mask_row(t, 1, c)))
        got = jnp.dot(jnp.concatenate(stack, axis=0), dft_ref[c], preferred_element_type=jnp.float32)
        for t in range(group.count):
            ended = running[t] + got[2 * t * rows : (2 * t + 1) * rows]
            group.series[t, c] = ended
            cross = jnp.broadcast_to(group.mask_row(t, 2, c), (rows, LANES)) > 0.5
            running[t] = jnp.where(cross, got[(2 * t + 1) * rows : (2 * t + 2) * rows], ended)
        for write in beside.get(c, ()):
            write()
    for t in range(group.count):
        group.series[t, group.chunks] = running[t]

    chunk_of = [[group.chunk_of(t, p) for p in range(1, group.bins)] for t in range(group.count)]
    pairs = [pair for row in chunk_of for pair in zip(row, row[1:])]
    any_inside = functools.reduce(jnp.logical_or, [a == b for a, b in pairs])

    @pl.when(any_inside)
    def _():
        def one(i, _):
            t, p = i // (group.bins - 2), i % (group.bins - 2) + 1

            @pl.when(group.inside(t, p))
            def _():
                c = group.chunk_of(t, p)
                ids = lax.broadcasted_iota(jnp.int32, (1, LANES), 1) + c * CHUNK
                member = jnp.where((ids >= group.edge(t, p)) & (ids < group.edge(t, p + 1)), 1.0, 0.0)
                prod = masked(product(group, spectra_ref, t, c), member)
                group.series[t, group.chunks + p] = jnp.dot(prod, dft_ref[c], preferred_element_type=jnp.float32)

            return 0

        lax.fori_loop(0, len(pairs), one, 0)


def sums_at(group, t):
    chunk_of = [group.chunk_of(t, p) for p in range(1, group.bins)]
    places = [chunk_of[0]]
    for p in range(1, group.bins - 1):
        places.append(jnp.where(chunk_of[p - 1] == chunk_of[p], group.chunks + p, chunk_of[p]))
    return places + [group.chunks]


def test_values(group, t, places, start, out_ref):
    slots, bins = group.rows // 2, group.bins
    row = group.first + t
    chi = power = None
    for d in range(2):

        def spread(ref, p, d=d):
            return jnp.broadcast_to(ref[t, 2 * p + d : 2 * p + d + 1, :], (8, LANES))

        rows = pl.ds(d * slots + start, 8)
        series = [group.series[t, place, rows, :] for place in places]
        whole = functools.reduce(jnp.add, series)
        for p in range(bins):
            dev = series[p] - spread(group.frac, p) * whole
            term = dev * dev * spread(group.inv, p)
            chi = term if chi is None else chi + term
        term = whole * whole * spread(group.inv, bins)
        power = term if power is None else power + term
    chi = jnp.sum(chi, axis=1, keepdims=True)
    power = power + pltpu.roll(power, TIME_LAGS, 1)
    peak = jnp.max(power, axis=1, keepdims=True)
    out_ids = lax.broadcasted_iota(jnp.int32, (8, LANES), 1)
    out = jnp.where(out_ids == row, peak, out_ref[start : start + 8, :])
    out_ref[start : start + 8, :] = jnp.where(out_ids == row + group.splat.shape[1], chi, out)


def values_of(group, out_ref):
    writes = []
    for t in range(group.count):
        places = sums_at(group, t)
        writes += [
            functools.partial(test_values, group, t, places, start, out_ref) for start in range(0, group.rows // 2, 8)
        ]
    return writes


def begin_kernel(out_ref):
    out_ref[...] = jnp.zeros_like(out_ref)


def own_kernel(
    seg_count,
    _, other_ref, own_ref, tmpl_ref, psd_ref, dft_ref, order_ref, seg_ref, edge_ref,
    spectra_ref, splat_ref, mask_ref, out_ref,
    start_ref, residue_ref, series_ref, inv_ref, frac_ref,
):
    for p in range(splat_ref.shape[0]):
        splat_ref[p] = jnp.broadcast_to(edge_ref[:, p : p + 1], splat_ref.shape[1:])
    chunk_masks(splat_ref, mask_ref)
    seg_starts(seg_ref, start_ref, seg_count)
    inverse_order(order_ref, residue_ref, seg_count)
    arrange_strain(0, own_ref, psd_ref, spectra_ref, start_ref, residue_ref, seg_count)
    arrange_strain(1, other_ref, psd_ref, spectra_ref, start_ref, residue_ref, seg_count)
    first = lax.axis_index("bank") * tmpl_ref.shape[0]
    group = Group(tmpl_ref, first, splat_ref, series_ref, inv_ref, frac_ref, mask_ref)
    add_up(group, spectra_ref, psd_ref, dft_ref)
    out_ref[...] = jnp.zeros_like(out_ref)
    for write in values_of(group, out_ref):
        write()


def mid_kernel(source, old_source, tmpl_ref, spectra_ref, dft_ref, psd_ref, splat_ref, mask_ref, old, sums, out_ref):
    bank, count = lax.axis_index("bank"), tmpl_ref.shape[0]
    group = Group(tmpl_ref, (bank ^ source()) * count, splat_ref, *sums, mask_ref)
    beside = {}
    if old:
        out_ref[...] = old[3][...]
        writes = values_of(Group(None, (bank ^ old_source()) * count, splat_ref, *old[:3]), out_ref)
        beside = {n + 1: [write] for n, write in enumerate(writes)}
    add_up(group, spectra_ref, psd_ref, dft_ref, beside)


def last_kernel(
    seg_count, sources, tmpl_ref, spectra_ref, dft_ref, psd_ref, splat_ref, mask_ref, order_ref, seg_ref, old_sums,
    part_ref, out_refs, sums, all_ref, placed_ref, start_ref, residue_ref, place_ref,
):
    pair_slots = all_ref.shape[0] // seg_count
    seg_here = lax.axis_index("seg")
    core, chip = seg_here % 2, seg_here // 2

    def place():
        seg_starts(seg_ref, start_ref, seg_count)
        inverse_order(order_ref, residue_ref, seg_count)
        for m in range(seg_count // 2):
            for source in range(2):
                start, first = first_slot(start_ref, residue_ref, seg_count, m, core ^ source)
                stop = start_ref[chip * 2 + source + 1]
                live = (stop - start - first + seg_count - 1) // seg_count
                place_ref[4 * m + 2 * source] = (start + first) // seg_count
                place_ref[4 * m + 2 * source + 1] = live

    bank, count = lax.axis_index("bank"), tmpl_ref.shape[0]
    all_ref[...] = part_ref[...]
    placed_ref[...] = jnp.zeros_like(placed_ref)
    old = Group(None, (bank ^ sources[0]()) * count, splat_ref, *old_sums)
    group = Group(tmpl_ref, (bank ^ sources[1]()) * count, splat_ref, *sums, mask_ref)
    writes = values_of(old, all_ref)
    add_up(group, spectra_ref, psd_ref, dft_ref, {n + 1: [write] for n, write in enumerate([place] + writes)})
    for write in values_of(group, all_ref):
        write()
    lanes = lax.broadcasted_iota(jnp.int32, all_ref.shape, 1)
    scale = 1.0 / (TIME_LAGS * 2.0 * 2 * (group.bins - 1))
    all_ref[...] = jnp.where(lanes < splat_ref.shape[1], jnp.sqrt(all_ref[...]), all_ref[...] * scale)
    ids = lax.broadcasted_iota(jnp.int32, (pair_slots, LANES), 0)
    for m in range(seg_count // 2):
        for source in range(2):
            values = all_ref[pl.ds((m * 2 + (core ^ source)) * pair_slots, pair_slots), :]
            values = jnp.where(ids < place_ref[4 * m + 2 * source + 1], values, 0.0)
            placed_ref[m, pl.ds(place_ref[4 * m + 2 * source], pair_slots), :] = values
        out_refs[m][...] = placed_ref[m, :BLK_DEV]


def add_kernel(part_refs, peak_ref, chi_ref):
    tmpl_total = peak_ref.shape[1]
    rows = functools.reduce(jnp.add, [ref[...] for ref in part_refs])
    peak_ref[...] = rows[:, :tmpl_total]
    chi_ref[...] = rows[:, tmpl_total : 2 * tmpl_total]


def swap(x, axis, step):
    return lax.ppermute(x, axis, [(i, i ^ step) for i in range(lax.axis_size(axis))])


def body(strain, templates, inv_psd, seg_blocks, dest_order, bin_edges):
    seg_count, bank_count = lax.axis_size("seg"), lax.axis_size("bank")
    chip_count = seg_count // 2
    slots, detectors, width = strain.shape
    freq_count = width // 2
    tmpl_total, bins = bin_edges.shape[0], bin_edges.shape[1] - 1
    tmpl_count = templates.shape[0]
    rows = detectors * slots
    tiles = detectors * width // LANES
    f32, i32 = jnp.float32, jnp.int32
    dft = jnp.asarray(dft_chunks(freq_count))
    psd = tile_rows(inv_psd)

    def shape(*dims, dtype=f32):
        return jax.ShapeDtypeStruct(dims, dtype)

    chunks = freq_count // CHUNK
    sums = [(tmpl_count, chunks + bins - 1, rows, 2 * TIME_LAGS)] + [(tmpl_count, 2 * bins + 8, LANES)] * 2
    sum_shapes = tuple(shape(*dims) for dims in sums)
    tables = [pltpu.SMEM((seg_count + 1,), i32), pltpu.SMEM((seg_count,), i32)]

    def call(kernel, name, flops, bytes_accessed=4 * 10**6, **kwargs):
        return pl.pallas_call(
            kernel,
            name=name,
            cost_estimate=pl.CostEstimate(flops=flops, bytes_accessed=bytes_accessed, transcendentals=0),
            compiler_params=pltpu.CompilerParams(vmem_limit_bytes=40 * 1024 * 1024),
            **kwargs,
        )

    begin = call(begin_kernel, "begin", 2 * 10**9, 1, out_shape=shape(8, LANES), out_specs=VMEM)()
    other = tile_rows(swap(strain, "seg", 1))
    def fetch(x, step):
        here = [(b, s) for b in range(bank_count) for s in range(seg_count)]
        return lax.ppermute(x, ("bank", "seg"), [((b ^ step(s)) * seg_count + (s ^ 1), b * seg_count + s) for b, s in here])

    far = [tile_rows(fetch(templates, lambda _, n=n: n)) for n in range(3, bank_count)]
    near = fetch(templates, lambda s: 2 - s % 2)

    splat_shape = shape(bins + 1, tmpl_total, LANES, dtype=i32)
    spectra, splat, mask, out = call(
        functools.partial(own_kernel, seg_count),
        "own_templates",
        10**9,
        out_shape=(shape((slots + 1) * tiles, LANES), splat_shape)
        + (shape(tmpl_total, 3, chunks, LANES), shape(slots, LANES)),
        in_specs=[VMEM] * 9,
        out_specs=(VMEM,) * 4,
        scratch_shapes=tables + [pltpu.VMEM(dims, f32) for dims in sums],
    )(begin, other, tile_rows(strain), tile_rows(templates), psd, dft, dest_order, seg_blocks, bin_edges)

    near, spectra = lax.optimization_barrier((near, spectra))
    held = (spectra, dft, psd, splat, mask)
    sources = [lambda: 2 - core_here(), lambda: 1 + core_here()]
    sources += [functools.partial(int, s) for s in range(3, bank_count)]
    remote = [[tile_rows(near)], [tile_rows(swap(part, "seg", 1)) for part in (near[:2], near[2:])]]
    remote += [[x] for x in far]
    old = []
    for n, parts in enumerate(remote[:-1]):

        def mid(*refs, n=n, count=len(old), split=len(parts)):
            parts, refs = refs[:split], refs[split:]
            ins, olds, (*outs, tmpl_ref) = refs[:5], refs[5 : 5 + count], refs[5 + count :]
            if split > 1:
                row = 0
                for ref in parts:
                    tmpl_ref[row : row + ref.shape[0]] = ref[...]
                    row += ref.shape[0]
            else:
                (tmpl_ref,) = parts
            out_ref = outs[3] if olds else None
            mid_kernel(sources[n], sources[n - 1], tmpl_ref, *ins, olds, outs[:3], out_ref)

        outs = sum_shapes + ((shape(slots, LANES),) if old else ())
        new = call(
            mid,
            "mid_templates" if old else "next_templates",
            1,
            1,
            out_shape=outs,
            in_specs=[VMEM] * (5 + len(parts) + len(old)),
            out_specs=(VMEM,) * len(outs),
            scratch_shapes=[pltpu.VMEM((tmpl_count, tiles, LANES), f32)],
        )(*parts, *held, *old)
        old = list(new) if old else [*new, out]

    def last(*refs):
        ins, sums_in, part_ref, refs = refs[:8], refs[8:11], refs[11], refs[12:]
        outs, refs = refs[:chip_count], refs[chip_count:]
        last_kernel(seg_count, sources[-2:], *ins, sums_in, part_ref, outs, refs[:3], *refs[3:])

    parts = call(
        last,
        "last_templates",
        10**9,
        out_shape=(shape(BLK_DEV, LANES),) * chip_count,
        in_specs=[VMEM] * 12,
        out_specs=(VMEM,) * chip_count,
        scratch_shapes=[pltpu.VMEM(dims, f32) for dims in sums]
        + [pltpu.VMEM((slots, LANES), f32), pltpu.VMEM((chip_count, BLK_DEV + 8, LANES), f32)]
        + tables
        + [pltpu.SMEM((4 * chip_count,), i32)],
    )(*remote[-1], *held, dest_order, seg_blocks, *old)

    got = [swap(parts[m], "seg", 2 * m + 1) for m in reversed(range(1, chip_count))] + [parts[0]]
    return call(
        lambda *refs: add_kernel(refs[:chip_count], *refs[chip_count:]),
        "add_rows",
        10**5,
        out_shape=(shape(BLK_DEV, tmpl_total),) * 2,
        in_specs=[VMEM] * chip_count,
        out_specs=(VMEM, VMEM),
    )(*got)


def solution(mesh):
    return jax.shard_map(
        body,
        mesh=mesh,
        in_specs=(
            P(("bank", "seg"), None, None),
            P("bank", None, None),
            P(),
            P("bank", None),
            P("bank", None),
            P(),
        ),
        out_specs=(P(("bank", "seg"), None), P(("bank", "seg"), None)),
        check_vma=False,
    )
```

```python
import functools

import jax
import jax.numpy as jnp
import ml_dtypes
import numpy as np
from jax import lax
from jax.experimental import pallas as pl
from jax.experimental.pallas import tpu as pltpu
from jax.sharding import PartitionSpec as P

TIME_LAGS = 64
BLK_DEV = 16
CHUNK = 128
LANES = 128
VMEM = pl.BlockSpec(memory_space=pltpu.VMEM)
SMEM = pl.BlockSpec(memory_space=pltpu.SMEM)


def dft_chunks(freq_count):
    turns = np.arange(freq_count)[:, None] * np.arange(TIME_LAGS)[None, :] % (2 * freq_count)
    angle = turns * (np.pi / freq_count)
    cosine, sine = np.cos(angle), np.sin(angle)
    upper = np.concatenate([cosine, sine], axis=1).reshape(-1, CHUNK, 2 * TIME_LAGS)
    lower = np.concatenate([-sine, cosine], axis=1).reshape(-1, CHUNK, 2 * TIME_LAGS)
    return np.concatenate([upper, lower], axis=1).astype(np.float32).astype(ml_dtypes.bfloat16)


def tile_rows(x):
    lead, (detectors, width) = x.shape[:-2], x.shape[-2:]
    tiles = jnp.swapaxes(x.reshape(lead + (detectors, width // LANES, LANES)), -3, -2)
    return tiles.reshape(lead + (detectors * width // LANES, LANES))


def core_here():
    return lax.axis_index("seg") % 2


def seg_starts(seg_ref, start_ref, seg_count):
    total = jnp.int32(0)
    for s in range(seg_count):
        start_ref[s] = total
        total = total + seg_ref[:, s : s + 1][0, 0]
    start_ref[seg_count] = total


def inverse_order(order_ref, residue_ref, seg_count):
    for r in range(seg_count):
        residue_ref[order_ref[:, r : r + 1][0, 0]] = jnp.int32(r)


def first_slot(start_ref, residue_ref, seg_count, m, side):
    seg_here = lax.axis_index("seg")
    core, chip = seg_here % 2, seg_here // 2
    start = start_ref[chip * 2 + (core ^ side)]
    residue = residue_ref[(chip ^ m) * 2 + (core ^ (m > 0))]
    return start, (residue - start % seg_count + seg_count) % seg_count


def arrange_strain(side, src_ref, psd_ref, spectra_ref, start_ref, residue_ref, seg_count):
    slots, tiles = src_ref.shape[0], src_ref.shape[1]
    pair_slots = slots // seg_count
    psd = psd_ref[...]
    both = jnp.concatenate([psd, psd], axis=0)
    for m in range(seg_count // 2):
        _, first = first_slot(start_ref, residue_ref, seg_count, m, side)
        for j in range(pair_slots):
            row = (m * 2 + side) * pair_slots + j
            spectra_ref[pl.ds(row, tiles, stride=slots + 1), :] = src_ref[first + j * seg_count].astype(jnp.float32) * both


def chunk_masks(splat_ref, mask_ref):
    shape = mask_ref.shape[2:]
    lanes = lax.broadcasted_iota(jnp.int32, shape, 1)
    starts = lax.broadcasted_iota(jnp.int32, shape, 0) * CHUNK
    for t in range(mask_ref.shape[0]):
        low = high = jnp.full(shape, CHUNK, jnp.int32)
        past = [jnp.broadcast_to(splat_ref[p, t : t + 1, :], shape) - starts for p in range(1, splat_ref.shape[0] - 1)]
        here = [(q >= 0) & (q < CHUNK) for q in past]
        for q, inside in zip(past, here):
            high = jnp.where(inside, q, high)
        for q, inside in zip(reversed(past), reversed(here)):
            low = jnp.where(inside, q, low)
        mask_ref[t, 0] = jnp.where(lanes < low, 1.0, 0.0)
        mask_ref[t, 1] = jnp.where(lanes >= high, 1.0, 0.0)
        mask_ref[t, 2] = jnp.where(high < CHUNK, 1.0, 0.0)


def sigma_rows(group, t, psd_ref):
    bins = group.bins
    tmpl = group.tmpl[t]
    half = tmpl.shape[0] // 2
    power = (tmpl[:half] * tmpl[:half] + tmpl[half:] * tmpl[half:]) * psd_ref[...]
    shape = power.shape
    ids = lax.broadcasted_iota(jnp.int32, shape, 0) // 2 * LANES + lax.broadcasted_iota(jnp.int32, shape, 1)
    below = [ids < group.edge_rows(t, p, shape) for p in range(1, bins)]
    row_pair = lax.broadcasted_iota(jnp.int32, (8, LANES), 0) // 2
    packs = []
    for p in range(bins):
        if p == 0:
            member = below[0]
        elif p == bins - 1:
            member = ~below[p - 1]
        else:
            member = below[p] & ~below[p - 1]
        part = jnp.where(member, power, 0.0)
        part = functools.reduce(jnp.add, [part[i : i + 8] for i in range(0, half, 8)])
        part = part + pltpu.roll(part, 4, 0)
        part = part + pltpu.roll(part, 2, 0)
        if p % 4 == 0:
            packs.append(part)
        else:
            packs[-1] = jnp.where(row_pair == p % 4, part, packs[-1])
    packs = [jnp.broadcast_to(jnp.sum(x, axis=1, keepdims=True), (8, LANES)) for x in packs]
    total = functools.reduce(jnp.add, packs)
    total = total + pltpu.roll(total, 4, 0)
    total = 1.0 / (total + pltpu.roll(total, 2, 0))
    for i, pack in enumerate(packs):
        group.inv[t, 8 * i : 8 * i + 8] = 1.0 / pack
        group.frac[t, 8 * i : 8 * i + 8] = pack * total
    group.inv[t, 2 * bins : 2 * bins + 8] = total


class Group:
    def __init__(self, tmpl_ref, first, splat_ref, series_ref, inv_ref, frac_ref, mask_ref=None):
        self.tmpl, self.first, self.splat = tmpl_ref, first, splat_ref
        self.series, self.inv, self.frac, self.mask = series_ref, inv_ref, frac_ref, mask_ref
        self.count, self.rows, self.bins = series_ref.shape[0], series_ref.shape[2], splat_ref.shape[0] - 1
        self.chunks = series_ref.shape[1] - (self.bins - 1)

    def edge_rows(self, t, p, shape):
        return jnp.broadcast_to(self.splat[p, pl.ds(self.first + t, 1), :], shape)

    def mask_row(self, t, kind, c):
        return self.mask[self.first + t, kind, c : c + 1, :]

    def edge(self, t, p):
        return self.splat[p, pl.ds(self.first + t, 1), :][0, 0]

    def chunk_of(self, t, p):
        return lax.shift_right_logical(self.edge(t, p), CHUNK.bit_length() - 1)

    def inside(self, t, p):
        return self.chunk_of(t, p) == self.chunk_of(t, p + 1)


def product(group, spectra_ref, t, chunk):
    slots = group.rows // 2

    def rows_of(ref, start, step, count):
        parts = [ref[pl.ds(start + d * step, count), :] for d in range(2)]
        return jnp.concatenate([jnp.broadcast_to(part, (slots, LANES)) for part in parts], axis=0)

    tiles = (chunk, group.chunks + chunk)
    tmpl_re, tmpl_im = (rows_of(group.tmpl.at[t], tile * 2, 1, 1) for tile in tiles)
    strain_re, strain_im = (rows_of(spectra_ref, tile * 2 * (slots + 1), slots + 1, slots) for tile in tiles)
    prod_re = tmpl_re * strain_re + tmpl_im * strain_im
    prod_im = tmpl_re * strain_im - tmpl_im * strain_re
    return jnp.concatenate([prod_re, prod_im], axis=1).astype(jnp.bfloat16)


def masked(prod, member):
    member = jnp.broadcast_to(member, (16, LANES)).astype(jnp.bfloat16)
    member = jnp.concatenate([member] * (prod.shape[0] // 16), axis=0)
    return prod * jnp.concatenate([member, member], axis=1)


def add_up(group, spectra_ref, psd_ref, dft_ref, beside=()):
    for t in range(group.count):
        sigma_rows(group, t, psd_ref)
    rows = group.rows
    beside = dict(beside)
    running = [jnp.zeros((rows, 2 * TIME_LAGS), jnp.float32) for _ in range(group.count)]
    for c in range(group.chunks):
        stack = []
        for t in range(group.count):
            prod = product(group, spectra_ref, t, c)
            stack.append(masked(prod, group.mask_row(t, 0, c)))
            stack.append(masked(prod, group.mask_row(t, 1, c)))
        got = jnp.dot(jnp.concatenate(stack, axis=0), dft_ref[c], preferred_element_type=jnp.float32)
        for t in range(group.count):
            ended = running[t] + got[2 * t * rows : (2 * t + 1) * rows]
            group.series[t, c] = ended
            cross = jnp.broadcast_to(group.mask_row(t, 2, c), (rows, LANES)) > 0.5
            running[t] = jnp.where(cross, got[(2 * t + 1) * rows : (2 * t + 2) * rows], ended)
        for write in beside.get(c, ()):
            write()
    for t in range(group.count):
        group.series[t, group.chunks] = running[t]

    chunk_of = [[group.chunk_of(t, p) for p in range(1, group.bins)] for t in range(group.count)]
    pairs = [pair for row in chunk_of for pair in zip(row, row[1:])]
    any_inside = functools.reduce(jnp.logical_or, [a == b for a, b in pairs])

    @pl.when(any_inside)
    def _():
        def one(i, _):
            t, p = i // (group.bins - 2), i % (group.bins - 2) + 1

            @pl.when(group.inside(t, p))
            def _():
                c = group.chunk_of(t, p)
                ids = lax.broadcasted_iota(jnp.int32, (1, LANES), 1) + c * CHUNK
                member = jnp.where((ids >= group.edge(t, p)) & (ids < group.edge(t, p + 1)), 1.0, 0.0)
                prod = masked(product(group, spectra_ref, t, c), member)
                group.series[t, group.chunks + p] = jnp.dot(prod, dft_ref[c], preferred_element_type=jnp.float32)

            return 0

        lax.fori_loop(0, len(pairs), one, 0)


def sums_at(group, t):
    chunk_of = [group.chunk_of(t, p) for p in range(1, group.bins)]
    places = [chunk_of[0]]
    for p in range(1, group.bins - 1):
        places.append(jnp.where(chunk_of[p - 1] == chunk_of[p], group.chunks + p, chunk_of[p]))
    return places + [group.chunks]


def test_values(group, t, places, start, out_ref):
    slots, bins = group.rows // 2, group.bins
    row = group.first + t
    chi = power = None
    for d in range(2):

        def spread(ref, p, d=d):
            return jnp.broadcast_to(ref[t, 2 * p + d : 2 * p + d + 1, :], (8, LANES))

        rows = pl.ds(d * slots + start, 8)
        series = [group.series[t, place, rows, :] for place in places]
        whole = functools.reduce(jnp.add, series)
        for p in range(bins):
            dev = series[p] - spread(group.frac, p) * whole
            term = dev * dev * spread(group.inv, p)
            chi = term if chi is None else chi + term
        term = whole * whole * spread(group.inv, bins)
        power = term if power is None else power + term
    chi = jnp.sum(chi, axis=1, keepdims=True)
    power = power + pltpu.roll(power, TIME_LAGS, 1)
    peak = jnp.max(power, axis=1, keepdims=True)
    out_ids = lax.broadcasted_iota(jnp.int32, (8, LANES), 1)
    out = jnp.where(out_ids == row, peak, out_ref[start : start + 8, :])
    out_ref[start : start + 8, :] = jnp.where(out_ids == row + group.splat.shape[1], chi, out)


def values_of(group, out_ref):
    writes = []
    for t in range(group.count):
        places = sums_at(group, t)
        writes += [
            functools.partial(test_values, group, t, places, start, out_ref) for start in range(0, group.rows // 2, 8)
        ]
    return writes


def begin_kernel(out_ref):
    out_ref[...] = jnp.zeros_like(out_ref)


def own_kernel(
    seg_count,
    _, other_ref, own_ref, tmpl_ref, psd_ref, dft_ref, order_ref, seg_ref, edge_ref,
    spectra_ref, splat_ref, mask_ref, out_ref,
    start_ref, residue_ref, series_ref, inv_ref, frac_ref,
):
    for p in range(splat_ref.shape[0]):
        splat_ref[p] = jnp.broadcast_to(edge_ref[:, p : p + 1], splat_ref.shape[1:])
    chunk_masks(splat_ref, mask_ref)
    seg_starts(seg_ref, start_ref, seg_count)
    inverse_order(order_ref, residue_ref, seg_count)
    arrange_strain(0, own_ref, psd_ref, spectra_ref, start_ref, residue_ref, seg_count)
    arrange_strain(1, other_ref, psd_ref, spectra_ref, start_ref, residue_ref, seg_count)
    first = lax.axis_index("bank") * tmpl_ref.shape[0]
    group = Group(tmpl_ref, first, splat_ref, series_ref, inv_ref, frac_ref, mask_ref)
    add_up(group, spectra_ref, psd_ref, dft_ref)
    out_ref[...] = jnp.zeros_like(out_ref)
    for write in values_of(group, out_ref):
        write()


def mid_kernel(source, old_source, tmpl_ref, spectra_ref, dft_ref, psd_ref, splat_ref, mask_ref, old, sums, out_ref):
    bank, count = lax.axis_index("bank"), tmpl_ref.shape[0]
    group = Group(tmpl_ref, (bank ^ source()) * count, splat_ref, *sums, mask_ref)
    beside = {}
    if old:
        out_ref[...] = old[3][...]
        writes = values_of(Group(None, (bank ^ old_source()) * count, splat_ref, *old[:3]), out_ref)
        beside = {n + 1: [write] for n, write in enumerate(writes)}
    add_up(group, spectra_ref, psd_ref, dft_ref, beside)


def last_kernel(
    seg_count, sources, tmpl_ref, spectra_ref, dft_ref, psd_ref, splat_ref, mask_ref, order_ref, seg_ref, old_sums,
    part_ref, out_refs, sums, all_ref, placed_ref, start_ref, residue_ref, place_ref,
):
    pair_slots = all_ref.shape[0] // seg_count
    seg_here = lax.axis_index("seg")
    core, chip = seg_here % 2, seg_here // 2

    def place():
        seg_starts(seg_ref, start_ref, seg_count)
        inverse_order(order_ref, residue_ref, seg_count)
        for m in range(seg_count // 2):
            for source in range(2):
                start, first = first_slot(start_ref, residue_ref, seg_count, m, core ^ source)
                stop = start_ref[chip * 2 + source + 1]
                live = (stop - start - first + seg_count - 1) // seg_count
                place_ref[4 * m + 2 * source] = (start + first) // seg_count
                place_ref[4 * m + 2 * source + 1] = live

    bank, count = lax.axis_index("bank"), tmpl_ref.shape[0]
    all_ref[...] = part_ref[...]
    placed_ref[...] = jnp.zeros_like(placed_ref)
    old = Group(None, (bank ^ sources[0]()) * count, splat_ref, *old_sums)
    group = Group(tmpl_ref, (bank ^ sources[1]()) * count, splat_ref, *sums, mask_ref)
    writes = values_of(old, all_ref)
    add_up(group, spectra_ref, psd_ref, dft_ref, {n + 1: [write] for n, write in enumerate([place] + writes)})
    for write in values_of(group, all_ref):
        write()
    lanes = lax.broadcasted_iota(jnp.int32, all_ref.shape, 1)
    scale = 1.0 / (TIME_LAGS * 2.0 * 2 * (group.bins - 1))
    all_ref[...] = jnp.where(lanes < splat_ref.shape[1], jnp.sqrt(all_ref[...]), all_ref[...] * scale)
    ids = lax.broadcasted_iota(jnp.int32, (pair_slots, LANES), 0)
    for m in range(seg_count // 2):
        for source in range(2):
            values = all_ref[pl.ds((m * 2 + (core ^ source)) * pair_slots, pair_slots), :]
            values = jnp.where(ids < place_ref[4 * m + 2 * source + 1], values, 0.0)
            placed_ref[m, pl.ds(place_ref[4 * m + 2 * source], pair_slots), :] = values
        out_refs[m][...] = placed_ref[m, :BLK_DEV]


def add_kernel(part_refs, peak_ref, chi_ref):
    tmpl_total = peak_ref.shape[1]
    rows = functools.reduce(jnp.add, [ref[...] for ref in part_refs])
    peak_ref[...] = rows[:, :tmpl_total]
    chi_ref[...] = rows[:, tmpl_total : 2 * tmpl_total]


def swap(x, axis, step):
    return lax.ppermute(x, axis, [(i, i ^ step) for i in range(lax.axis_size(axis))])


def body(strain, templates, inv_psd, seg_blocks, dest_order, bin_edges):
    seg_count, bank_count = lax.axis_size("seg"), lax.axis_size("bank")
    chip_count = seg_count // 2
    slots, detectors, width = strain.shape
    freq_count = width // 2
    tmpl_total, bins = bin_edges.shape[0], bin_edges.shape[1] - 1
    tmpl_count = templates.shape[0]
    rows = detectors * slots
    tiles = detectors * width // LANES
    f32, i32 = jnp.float32, jnp.int32
    dft = jnp.asarray(dft_chunks(freq_count))
    psd = tile_rows(inv_psd)

    def shape(*dims, dtype=f32):
        return jax.ShapeDtypeStruct(dims, dtype)

    chunks = freq_count // CHUNK
    sums = [(tmpl_count, chunks + bins - 1, rows, 2 * TIME_LAGS)] + [(tmpl_count, 2 * bins + 8, LANES)] * 2
    sum_shapes = tuple(shape(*dims) for dims in sums)
    tables = [pltpu.SMEM((seg_count + 1,), i32), pltpu.SMEM((seg_count,), i32)]

    def call(kernel, name, flops, bytes_accessed=4 * 10**6, **kwargs):
        return pl.pallas_call(
            kernel,
            name=name,
            cost_estimate=pl.CostEstimate(flops=flops, bytes_accessed=bytes_accessed, transcendentals=0),
            compiler_params=pltpu.CompilerParams(vmem_limit_bytes=40 * 1024 * 1024),
            **kwargs,
        )

    begin = call(begin_kernel, "begin", 2 * 10**9, 1, out_shape=shape(8, LANES), out_specs=VMEM)()
    other = tile_rows(swap(strain, "seg", 1))
    def fetch(x, step):
        here = [(b, s) for b in range(bank_count) for s in range(seg_count)]
        return lax.ppermute(x, ("bank", "seg"), [((b ^ step(s)) * seg_count + (s ^ 1), b * seg_count + s) for b, s in here])

    far = [tile_rows(fetch(templates, lambda _, n=n: n)) for n in range(3, bank_count)]
    near = fetch(templates, lambda s: 2 - s % 2)

    splat_shape = shape(bins + 1, tmpl_total, LANES, dtype=i32)
    spectra, splat, mask, out = call(
        functools.partial(own_kernel, seg_count),
        "own_templates",
        10**9,
        out_shape=(shape((slots + 1) * tiles, LANES), splat_shape)
        + (shape(tmpl_total, 3, chunks, LANES), shape(slots, LANES)),
        in_specs=[VMEM] * 9,
        out_specs=(VMEM,) * 4,
        scratch_shapes=tables + [pltpu.VMEM(dims, f32) for dims in sums],
    )(begin, other, tile_rows(strain), tile_rows(templates), psd, dft, dest_order, seg_blocks, bin_edges)

    near, spectra = lax.optimization_barrier((near, spectra))
    held = (spectra, dft, psd, splat, mask)
    sources = [lambda: 2 - core_here(), lambda: 1 + core_here()]
    sources += [functools.partial(int, s) for s in range(3, bank_count)]
    remote = [[tile_rows(near)], [tile_rows(swap(part, "seg", 1)) for part in (near[:2], near[2:])]]
    remote += [[x] for x in far]
    old = []
    for n, parts in enumerate(remote[:-1]):

        def mid(*refs, n=n, count=len(old), split=len(parts)):
            parts, refs = refs[:split], refs[split:]
            ins, olds, (*outs, tmpl_ref) = refs[:5], refs[5 : 5 + count], refs[5 + count :]
            if split > 1:
                row = 0
                for ref in parts:
                    tmpl_ref[row : row + ref.shape[0]] = ref[...]
                    row += ref.shape[0]
            else:
                (tmpl_ref,) = parts
            out_ref = outs[3] if olds else None
            mid_kernel(sources[n], sources[n - 1], tmpl_ref, *ins, olds, outs[:3], out_ref)

        outs = sum_shapes + ((shape(slots, LANES),) if old else ())
        new = call(
            mid,
            "mid_templates" if old else "next_templates",
            1,
            1,
            out_shape=outs,
            in_specs=[VMEM] * (5 + len(parts) + len(old)),
            out_specs=(VMEM,) * len(outs),
            scratch_shapes=[pltpu.VMEM((tmpl_count, tiles, LANES), f32)],
        )(*parts, *held, *old)
        old = list(new) if old else [*new, out]

    def last(*refs):
        ins, sums_in, part_ref, refs = refs[:8], refs[8:11], refs[11], refs[12:]
        outs, refs = refs[:chip_count], refs[chip_count:]
        last_kernel(seg_count, sources[-2:], *ins, sums_in, part_ref, outs, refs[:3], *refs[3:])

    parts = call(
        last,
        "last_templates",
        10**9,
        out_shape=(shape(BLK_DEV, LANES),) * chip_count,
        in_specs=[VMEM] * 12,
        out_specs=(VMEM,) * chip_count,
        scratch_shapes=[pltpu.VMEM(dims, f32) for dims in sums]
        + [pltpu.VMEM((slots, LANES), f32), pltpu.VMEM((chip_count, BLK_DEV + 8, LANES), f32)]
        + tables
        + [pltpu.SMEM((4 * chip_count,), i32)],
    )(*remote[-1], *held, dest_order, seg_blocks, *old)

    order = [*range(2, chip_count), 1]
    got = [swap(parts[m], "seg", 2 * m + 1) for m in order] + [parts[0]]
    return call(
        lambda *refs: add_kernel(refs[:chip_count], *refs[chip_count:]),
        "add_rows",
        10**5,
        out_shape=(shape(BLK_DEV, tmpl_total),) * 2,
        in_specs=[VMEM] * chip_count,
        out_specs=(VMEM, VMEM),
    )(*got)


def solution(mesh):
    return jax.shard_map(
        body,
        mesh=mesh,
        in_specs=(
            P(("bank", "seg"), None, None),
            P("bank", None, None),
            P(),
            P("bank", None),
            P("bank", None),
            P(),
        ),
        out_specs=(P(("bank", "seg"), None), P(("bank", "seg"), None)),
        check_vma=False,
    )
```
